512 devices in a mesh: tm: 8 (over x, y_hi), array: 64 (over z, y_lo, core).
Axes of the slice: x: 4, y: 4 (y_hi: 2, y_lo: 2; y = y_hi * 2 + y_lo), z: 16, core: 2. Of those that a mesh axis runs over, the one named last changes fastest.
Arguments:
- raw_strain: bfloat16 [8, 8192, 1024], P('tm', 'array'), may hold values from -6 to 6
- fir_taps: float32 [8], replicated, may hold values from -3 to 3
- source_ids: int32 [4, 32], replicated, may hold values from 0 to 8191, as said below
Outputs:
- stacked: bfloat16 [128, 101, 8192], P('tm', None, 'array')
The draws below stay inside these ranges and needn't reach their ends.
Inputs may be any that keep to these rules, and one draw needn't show every extreme that they name: `source_ids`: channel ids of the virtual sources.
All inputs are finite; a program needn't handle non-finite values.
Results may differ from the reference program's by a relative error of at most 0.017.
Values may be sent and summed in bfloat16 or wider, within the bound.
A program may use at most 128 MiB of HBM per device.

```python
import math
import jax
import jax.numpy as jnp
from jax import lax

CH = 8192
SOURCES = 128
ROUNDS = 4
MAXLAG = 50
WINDOW = 64
DECIM = 4
NTAP = 8
SAMPLES = 256
SRC_ROUND = 32
LAGS = 101
RAW = 1024
SEGMENTS = 8


def draw_source_ids(key, part):
    key = jax.random.fold_in(key, 7)
    picked = jax.random.randint(key, (ROUNDS, SRC_ROUND), 0, CH, dtype=jnp.int32)
    picked = picked.at[0, 0].set(0)
    picked = picked.at[ROUNDS - 1, SRC_ROUND - 1].set(CH - 1)
    return picked


def level_of(stream_key, dims, cuts, smallest, high):
    def one(position, parts):
        draws = jax.random.uniform(jax.random.fold_in(jax.random.fold_in(stream_key, 6), position), (parts,), jnp.float32, smallest / len(cuts), high / len(cuts))
        return jnp.repeat(jnp.exp(draws), dims[position] // parts).reshape((-1,) + (1,) * (len(dims) - position - 1))

    loudness = one(*cuts[0])
    for cut in cuts[1:]:
        loudness = loudness * one(*cut)
    return loudness


def bell_draw(stream_key, extent, deviation, limit, cuts=(), kind=jnp.bfloat16):
    level = level_of(stream_key, extent, cuts, -0.22, 0.18) if cuts else 1.0
    values = jax.random.normal(stream_key, extent, jnp.float32) * deviation * level
    return jnp.minimum(jnp.maximum(values, -limit), limit).astype(kind)


def setup_inputs(seed: int = 0) -> dict:
    streams_of = jax.random.split(jax.random.key(seed), 4)
    raw_strain = bell_draw(streams_of[0], (SEGMENTS, CH, RAW), 1.0, 6.0, ((0, 8), (1, 64)))
    fir_taps = bell_draw(streams_of[1], (NTAP,), 0.5, 3.0, (), jnp.float32)
    source_ids = draw_source_ids(jax.random.fold_in(streams_of[3], 71), 0)
    return dict(raw_strain=raw_strain, fir_taps=fir_taps, source_ids=source_ids)


epsilon = 1e-05

def decimate(raw_segment, fir_taps):
    phases = [raw_segment[:, phase_index::DECIM] for phase_index in range(DECIM)]
    filtered = jnp.zeros((raw_segment.shape[0], SAMPLES), jnp.float32)
    for tap_index in range(NTAP):
        phase_index = -tap_index % DECIM
        delay = (tap_index + phase_index) // DECIM
        shifted = jnp.pad(phases[phase_index], ((0, 0), (delay, 0)))[:, :SAMPLES]
        filtered = filtered + fir_taps[tap_index] * shifted.astype(jnp.float32)
    return filtered

def normalize(filtered):
    half_window = WINDOW // 2
    window_sum = jnp.pad(jnp.abs(filtered), ((0, 0), (half_window, 0)))
    span_now = 1
    while span_now < WINDOW:
        window_sum = window_sum + jnp.pad(window_sum[:, span_now:], ((0, 0), (0, span_now)))
        span_now = span_now * 2
    window_sum = window_sum[:, :SAMPLES]
    return (filtered / (window_sum * (1.0 / WINDOW) + epsilon)).astype(jnp.bfloat16)

def reference(raw_strain, fir_taps, source_ids):
    flat_ids = source_ids.reshape(-1).astype(jnp.int32)
    running = jnp.zeros((SOURCES, LAGS, CH), jnp.float32)
    factor = 1.0 / math.sqrt(SAMPLES)
    for segment in range(SEGMENTS):
        normed = normalize(decimate(raw_strain[segment], fir_taps))
        source_rows = normed[flat_ids]
        padded = jnp.pad(source_rows, ((0, 0), (MAXLAG, MAXLAG)))
        lagged = jnp.stack([padded[:, 2 * MAXLAG - lag_index:2 * MAXLAG - lag_index + SAMPLES] for lag_index in range(LAGS)], 1)
        partial_value = jnp.einsum('slt,ct->slc', lagged.astype(jnp.float32), normed.astype(jnp.float32)) * factor
        running = running + lax.optimization_barrier(partial_value.astype(jnp.bfloat16)).astype(jnp.float32)
    return (running * (1.0 / math.sqrt(SEGMENTS))).astype(jnp.bfloat16)
```

```python
import functools
import math

import jax
import jax.numpy as jnp
from jax import lax
from jax.experimental import pallas as pl
from jax.experimental.pallas import tpu as pltpu
from jax.sharding import PartitionSpec as P

MESH = pl.DeviceIdType.MESH
SOURCES = 128
MAXLAG = 50
WINDOW = 64
DECIM = 4
NTAP = 8
SAMPLES = 256
LAGS = 101
RAW = 1024
SEG = 8
ROWS = 16
CH = 128
NZ = 16
NYC = 4
LPAD = 104
UP = 26
DOWN = 25
EPSILON = 1e-05
SCALE = 1.0 / (math.sqrt(SAMPLES) * math.sqrt(SEG))

f32 = jnp.float32
bf16 = jnp.bfloat16
NT = (((1,), (1,)), ((), ()))
TN = (((0,), (0,)), ((), ()))


def iota(shape, dim):
    return lax.broadcasted_iota(jnp.int32, shape, dim)


def terms(value, count):
    parts = []
    for _ in range(count):
        part = value.astype(bf16)
        parts.append(part)
        value = value - part.astype(f32)
    return parts


def normalize(raw, taps_ref):
    k = DECIM * iota((128, 128), 1) - iota((128, 128), 0)
    band = jnp.zeros((128, 128), f32)
    for tap in range(NTAP):
        band = jnp.where(k == tap, taps_ref[tap], band)
    band = jnp.concatenate([band, jnp.zeros((128, 128), f32)], 1)
    lane = iota((128, SAMPLES), 1)
    filtered = jnp.zeros((CH, SAMPLES), f32)
    for tile in range(RAW // 128):
        placed = pltpu.roll(band, 32 * tile, 1) if tile else band
        if tile == RAW // 128 - 1:
            placed = jnp.where(lane < 2, 0.0, placed)
        piece = raw[:, 128 * tile : 128 * (tile + 1)]
        for part in terms(placed, 3):
            filtered = filtered + jnp.dot(piece, part, preferred_element_type=f32)
    gap = iota((SAMPLES, SAMPLES), 0) - iota((SAMPLES, SAMPLES), 1)
    window = jnp.where((gap >= -(WINDOW // 2)) & (gap < WINDOW // 2), 1.0, 0.0).astype(bf16)
    total = jnp.zeros((CH, SAMPLES), f32)
    for part in terms(jnp.abs(filtered), 2):
        total = total + jnp.dot(part, window, preferred_element_type=f32)
    return filtered / (total * (1.0 / WINDOW) + EPSILON)


def kernel(
    raw_ref, taps_ref, ids_ref, out_ref,
    xall, send1, recv1, mine2, recv2, mine3, rows, lhs_up, lhs_down, corr,
    x_send, x_recv, s1_send, s1_recv, s2_send, s2_recv, s3_send, s3_recv,
):
    tm = lax.axis_index("tm")
    place = lax.axis_index("array")
    z = lax.div(place, NYC)
    yc = lax.rem(place, NYC)
    owner = lax.div(z, 2)
    half = lax.rem(z, 2)
    own = tm == owner

    def along_z(d):
        return {"tm": tm, "array": lax.rem(z + d, NZ) * NYC + yc}

    def along_yc(d):
        return {"tm": tm, "array": z * NYC + lax.rem(yc + d, NYC)}

    def along_tm(d):
        return {"tm": lax.rem(tm + d, SEG), "array": place}

    def to_owner(d):
        return {"tm": owner, "array": lax.rem(z + d, NZ) * NYC + yc}

    barrier = pltpu.get_barrier_semaphore()

    def greet(device):
        pl.semaphore_signal(barrier, inc=1, device_id=device, device_id_type=MESH)

    for d in range(1, NZ):
        greet(along_z(d))
    for d in range(1, NYC):
        greet(along_yc(d))
    for d in range(1, SEG):
        greet(along_tm(d))
    for g in range(SEG):
        for h in range(2):
            sender = {"tm": g, "array": (2 * tm + h) * NYC + yc}
            pl.when(jnp.logical_not((tm == g) & (z == 2 * tm + h)))(functools.partial(greet, sender))

    normed = normalize(raw_ref[0], taps_ref)
    xall[tm] = normed.astype(bf16)

    ids = jnp.concatenate([ids_ref[r : r + 1, :] for r in range(4)], 1)
    chosen = (iota((CH, SOURCES), 0) == ids - place * CH).astype(f32).astype(bf16)
    picked = lax.dot_general(chosen, xall[tm], TN, preferred_element_type=f32)
    for chunk in range(NZ):
        part = picked[8 * chunk : 8 * chunk + 8]
        send1[chunk] = jnp.concatenate([part[:, :128], part[:, 128:]], 0).astype(bf16)

    @pl.when(own)
    def _():
        pl.semaphore_wait(barrier, NZ - 1 + NYC - 1 + SEG - 1 + 15)

    @pl.when(jnp.logical_not(own))
    def _():
        pl.semaphore_wait(barrier, NZ - 1 + NYC - 1 + SEG - 1 + 16)

    first = [
        pltpu.make_async_remote_copy(
            send1.at[lax.rem(z + d, NZ)], recv1.at[d], s1_send.at[d], s1_recv.at[d], along_z(d), MESH
        )
        for d in range(1, NZ)
    ]
    for copy in first:
        copy.start()
    gather = [
        pltpu.make_async_remote_copy(
            xall.at[tm], xall.at[tm], x_send.at[d], x_recv.at[d], along_tm(d), MESH
        )
        for d in range(1, SEG)
    ]
    for copy in gather:
        copy.start()

    total = send1[z].astype(f32)
    for d in range(1, NZ):
        first[d - 1].wait_recv()
        total = total + recv1[d].astype(f32)
    mine2[...] = total.astype(bf16)
    second = [
        pltpu.make_async_remote_copy(
            mine2, recv2.at[d], s2_send.at[d], s2_recv.at[d], along_yc(d), MESH
        )
        for d in range(1, NYC)
    ]
    for copy in second:
        copy.start()
    for d in range(1, NYC):
        second[d - 1].wait_recv()
        total = total + recv2[d].astype(f32)
    mine3[...] = total.astype(bf16)

    slot = 2 * tm + half
    third = [
        pltpu.make_async_remote_copy(
            mine3, rows.at[slot], s3_send.at[d], s3_recv.at[slot], to_owner(d), MESH
        )
        for d in range(NZ)
    ]
    for copy in third[1:]:
        copy.start()
    here = pltpu.make_async_copy(mine3, rows.at[slot], s3_recv.at[slot])
    pl.when(own)(lambda: here.start())
    pl.when(jnp.logical_not(own))(lambda: third[0].start())

    for g in range(SEG):
        for h in range(2):
            pltpu.make_async_copy(rows.at[2 * g + h], rows.at[2 * g + h], s3_recv.at[2 * g + h]).wait()

    lane = iota((ROWS, 128), 1)
    for g in range(SEG):
        a = rows[2 * g].astype(f32)
        b = rows[2 * g + 1].astype(f32)
        low = jnp.concatenate([a[:8], b[:8]], 0)
        high = jnp.concatenate([a[8:], b[8:]], 0)
        for i in range(UP):
            q = 2 * i
            lo, hi = (pltpu.roll(low, q, 1), pltpu.roll(high, q, 1)) if q else (low, high)
            lhs_up[ROWS * i : ROWS * (i + 1), 256 * g : 256 * g + 128] = jnp.where(lane < q, 0.0, lo).astype(bf16)
            lhs_up[ROWS * i : ROWS * (i + 1), 256 * g + 128 : 256 * g + 256] = jnp.where(lane < q, lo, hi).astype(bf16)
        for i in range(DOWN):
            q = 128 - (2 * i + 1)
            lo, hi = pltpu.roll(low, q, 1), pltpu.roll(high, q, 1)
            lhs_down[ROWS * i : ROWS * (i + 1), 256 * g : 256 * g + 128] = jnp.where(lane < q, lo, hi).astype(bf16)
            lhs_down[ROWS * i : ROWS * (i + 1), 256 * g + 128 : 256 * g + 256] = jnp.where(lane < q, hi, 0.0).astype(bf16)

    for copy in gather:
        copy.wait_recv()

    wide = iota((CH, SAMPLES), 1)
    up = jnp.zeros((ROWS * UP, 256), f32)
    down = jnp.zeros((ROWS * DOWN, 256), f32)
    for g in range(SEG):
        x = xall[g]
        later = pltpu.roll(x.astype(f32), SAMPLES - 1, 1)
        later = jnp.where(wide == SAMPLES - 1, 0.0, later).astype(bf16)
        earlier = pltpu.roll(x.astype(f32), 1, 1)
        earlier = jnp.where(wide == 0, 0.0, earlier).astype(bf16)
        cols = slice(256 * g, 256 * g + 256)
        up = up + lax.dot_general(
            lhs_up[:, cols], jnp.concatenate([x, later], 0), NT, preferred_element_type=f32
        )
        down = down + lax.dot_general(
            lhs_down[:, cols], jnp.concatenate([x, earlier], 0), NT, preferred_element_type=f32
        )

    for i in range(UP):
        block = up[ROWS * i : ROWS * (i + 1)] * SCALE
        lag = MAXLAG + 2 * i
        corr[pl.ds(lag, ROWS, stride=LPAD), :] = block[:, :128]
        if lag + 1 < LAGS:
            corr[pl.ds(lag + 1, ROWS, stride=LPAD), :] = block[:, 128:]
    for i in range(DOWN):
        block = down[ROWS * i : ROWS * (i + 1)] * SCALE
        lag = MAXLAG - 1 - 2 * i
        corr[pl.ds(lag, ROWS, stride=LPAD), :] = block[:, :128]
        corr[pl.ds(lag - 1, ROWS, stride=LPAD), :] = block[:, 128:]
    for j in range(ROWS):
        out_ref[j] = corr[LPAD * j : LPAD * j + LAGS, :].astype(bf16)

    for copy in first + gather + second + third[1:]:
        copy.wait_send()
    pl.when(jnp.logical_not(own))(lambda: third[0].wait_send())


def body(raw_strain, fir_taps, source_ids):
    vmem = pl.BlockSpec(memory_space=pltpu.VMEM)
    dma = pltpu.SemaphoreType.DMA
    return pl.pallas_call(
        kernel,
        out_shape=jax.ShapeDtypeStruct((ROWS, LAGS, CH), bf16),
        in_specs=[vmem, pl.BlockSpec(memory_space=pltpu.SMEM), vmem],
        out_specs=vmem,
        scratch_shapes=[
            pltpu.VMEM((SEG, CH, SAMPLES), bf16),
            pltpu.VMEM((NZ, 16, 128), bf16),
            pltpu.VMEM((NZ, 16, 128), bf16),
            pltpu.VMEM((16, 128), bf16),
            pltpu.VMEM((NYC, 16, 128), bf16),
            pltpu.VMEM((16, 128), bf16),
            pltpu.VMEM((2 * SEG, 16, 128), bf16),
            pltpu.VMEM((ROWS * UP, SEG * SAMPLES), bf16),
            pltpu.VMEM((ROWS * DOWN, SEG * SAMPLES), bf16),
            pltpu.VMEM((ROWS * LPAD, CH), f32),
            dma((SEG,)), dma((SEG,)),
            dma((NZ,)), dma((NZ,)),
            dma((NYC,)), dma((NYC,)),
            dma((NZ,)), dma((2 * SEG,)),
        ],
        compiler_params=pltpu.CompilerParams(
            collective_id=0, has_side_effects=True, vmem_limit_bytes=40 * 1024 * 1024
        ),
    )(raw_strain, fir_taps, source_ids)


def solution(mesh):
    return jax.shard_map(
        body,
        mesh=mesh,
        in_specs=(P("tm", "array", None), P(), P()),
        out_specs=P("tm", None, "array"),
        check_vma=False,
    )
```

```python
import functools
import math

import jax
import jax.numpy as jnp
from jax import lax
from jax.experimental import pallas as pl
from jax.experimental.pallas import tpu as pltpu
from jax.sharding import PartitionSpec as P

MESH = pl.DeviceIdType.MESH
SOURCES = 128
MAXLAG = 50
WINDOW = 64
DECIM = 4
NTAP = 8
SAMPLES = 256
LAGS = 101
RAW = 1024
SEG = 8
ROWS = 16
CH = 128
NZ = 16
NYC = 4
NEAR = 4
UP = 26
DOWN = 25
EPSILON = 1e-05
SCALE = 1.0 / (math.sqrt(SAMPLES) * math.sqrt(SEG))

f32 = jnp.float32
bf16 = jnp.bfloat16
TN = (((0,), (0,)), ((), ()))


def iota(shape, dim):
    return lax.broadcasted_iota(jnp.int32, shape, dim)


def terms(value, count):
    parts = []
    for _ in range(count):
        part = value.astype(bf16)
        parts.append(part)
        value = value - part.astype(f32)
    return parts


def tap_bands(taps_ref):
    k = DECIM * iota((128, 128), 1) - iota((128, 128), 0)
    band = jnp.zeros((128, 128), f32)
    for tap in range(NTAP):
        band = jnp.where(k == tap, taps_ref[tap], band)
    band = jnp.concatenate([band, jnp.zeros((128, 128), f32)], 1)
    lane = iota((128, SAMPLES), 1)
    bands = []
    for tile in range(RAW // 128):
        placed = pltpu.roll(band, 32 * tile, 1) if tile else band
        if tile == RAW // 128 - 1:
            placed = jnp.where(lane < 2, 0.0, placed)
        bands.append(terms(placed, 3))
    return bands


def normalize(raw, bands):
    filtered = jnp.zeros((CH, SAMPLES), f32)
    for term in range(3):
        matrix = jnp.concatenate([band[term] for band in bands], 0)
        filtered = filtered + jnp.dot(raw, matrix, preferred_element_type=f32)
    gap = iota((SAMPLES, SAMPLES), 0) - iota((SAMPLES, SAMPLES), 1)
    window = jnp.where((gap >= -(WINDOW // 2)) & (gap < WINDOW // 2), 1.0, 0.0).astype(bf16)
    total = jnp.zeros((CH, SAMPLES), f32)
    for part in terms(jnp.abs(filtered), 2):
        total = total + jnp.dot(part, window, preferred_element_type=f32)
    return filtered / (total * (1.0 / WINDOW) + EPSILON)


def kernel(
    raw_hbm, taps_hbm, ids_hbm, out_ref,
    raw, taps, ids_ref, xall, send1, recv1, mine2, recv2, mine3, parts, rows, lhs_up, lhs_down, rhs_up, rhs_down,
    in_sem, x_send, x_recv, s1_send, s1_recv, s2_send, s2_recv, s3_send, s3_recv, s4_send, s4_recv, column, ready,
):
    inputs = [
        pltpu.make_async_copy(src, dst, in_sem.at[i])
        for i, (src, dst) in enumerate(((taps_hbm, taps), (raw_hbm, raw), (ids_hbm, ids_ref)))
    ]
    for copy in inputs:
        copy.start()

    tm = lax.axis_index("tm")
    place = lax.axis_index("array")
    z = lax.div(place, NYC)
    yc = lax.rem(place, NYC)
    core = lax.rem(place, 2)
    owner = lax.rem(z, SEG)
    own = tm == owner

    def at(t, dz, side):
        return {"tm": t, "array": lax.rem(z + dz + NZ, NZ) * NYC + side}

    def along_z(d):
        return at(tm, d, yc)

    yc_peer = [None, yc + 1 - 2 * core, lax.rem(yc + 2, NYC), lax.rem(yc + 2, NYC) + 1 - 2 * core]

    def along_yc(d):
        return at(tm, 0, yc_peer[d])

    def along_tm(d):
        return at(lax.rem(tm + d, SEG), 0, yc)

    near = [-4, 4, -3, 3, -2, 2, -1, 1]
    barrier = pltpu.get_barrier_semaphore()

    def signal(semaphore, device):
        pl.semaphore_signal(semaphore, inc=1, device_id=device, device_id_type=MESH)

    for d in near:
        signal(barrier, along_z(d))
    for d in range(1, SEG):
        signal(barrier, along_tm(d))
    for d in range(1, NYC):
        signal(barrier, along_yc(d))

    inputs[0].wait()
    bands = tap_bands(taps)
    inputs[1].wait()
    normed = normalize(raw[0], bands)
    xall[tm] = normed.astype(bf16)

    inputs[2].wait()
    ids = jnp.concatenate([ids_ref[r : r + 1, :] for r in range(4)], 1)
    chosen = (iota((CH, SOURCES), 0) == ids - place * CH).astype(f32).astype(bf16)
    picked = lax.dot_general(chosen, xall[tm], TN, preferred_element_type=f32).astype(bf16)
    for t in range(SEG):
        for h in range(2):
            send1[t, h] = picked[ROWS * t : ROWS * (t + 1), 128 * h : 128 * (h + 1)]

    pl.semaphore_wait(barrier, len(near) + NYC - 1 + SEG - 1)

    spread = [d for d in near if d != 4]
    first = [
        pltpu.make_async_remote_copy(
            send1.at[lax.rem(z + d + NZ, SEG)], recv1.at[i], s1_send.at[i], s1_recv.at[i], along_z(d), MESH
        )
        for i, d in enumerate(spread)
    ]
    for copy in first:
        copy.start()
    signal(column, along_z(-4))
    signal(column, along_z(4))
    gather = [
        pltpu.make_async_remote_copy(
            xall.at[tm], xall.at[tm], x_send.at[d], x_recv.at[d], along_tm(d), MESH
        )
        for d in range(1, SEG)
    ]
    for copy in gather:
        copy.start()

    total = send1[owner].astype(f32)
    for i in reversed(range(len(spread))):
        first[i].wait_recv()
        total = total + recv1[i].astype(f32)
    mine2[...] = total.astype(bf16)

    second = [
        pltpu.make_async_remote_copy(
            mine2.at[core if d == 2 else 1 - core], recv2.at[d], s2_send.at[d], s2_recv.at[d], along_yc(d), MESH
        )
        for d in range(1, NYC)
    ]
    for copy in second:
        copy.start()

    pl.semaphore_wait(column, 2)

    @pl.when(own)
    def _():
        for d in range(1, SEG):
            signal(ready, along_tm(d))

    total = mine2[core].astype(f32)
    for d in range(1, NYC):
        second[d - 1].wait_recv()
        total = total + recv2[d].astype(f32)
    mine3[...] = total.astype(bf16)

    pl.when(jnp.logical_not(own))(lambda: pl.semaphore_wait(ready, 1))
    slot = 2 * tm + lax.div(z, SEG)
    third = [
        pltpu.make_async_remote_copy(
            mine3, parts.at[slot], s3_send.at[d], s3_recv.at[slot], at(owner, d, yc), MESH
        )
        for d in range(NZ)
    ]
    here = pltpu.make_async_copy(mine3, parts.at[slot], s3_recv.at[slot])
    for d in (8, 7, 9, 6, 10, 5, 11, 4, 12, 3, 13, 2, 14, 1, 15):
        third[d].start()
    pl.when(own)(lambda: here.start())
    pl.when(jnp.logical_not(own))(lambda: third[0].start())

    step = iota((SAMPLES, CH), 0)
    for g in range(SEG):
        if g:
            gather[g - 1].wait_recv()
    for g in range(SEG):
        x = xall[g].astype(f32).T
        later = jnp.where(step == SAMPLES - 1, 0.0, pltpu.roll(x, SAMPLES - 1, 0))
        earlier = jnp.where(step == 0, 0.0, pltpu.roll(x, 1, 0))
        span = slice(SAMPLES * g, SAMPLES * (g + 1))
        rhs_up[span, :CH] = x.astype(bf16)
        rhs_up[span, CH:] = later.astype(bf16)
        rhs_down[span, :CH] = x.astype(bf16)
        rhs_down[span, CH:] = earlier.astype(bf16)

    for g in range(SEG):
        for p in range(2):
            i = 2 * g + p
            pltpu.make_async_copy(parts.at[i], parts.at[i], s3_recv.at[i]).wait()
        rows[core, g] = (parts[2 * g].astype(f32) + parts[2 * g + 1].astype(f32)).astype(bf16)

    swap = pltpu.make_async_remote_copy(
        rows.at[core], rows.at[core], s4_send, s4_recv, along_yc(1), MESH
    )
    swap.start()
    swap.wait_recv()

    lane = iota((ROWS, 128), 1)
    for g in range(SEG):
        low = rows[0, g].astype(f32)
        high = rows[1, g].astype(f32)
        a, b, c = (slice(256 * g + 128 * i, 256 * g + 128 * i + 128) for i in range(3))
        for i in range(UP):
            q = 2 * i
            lo, hi = (pltpu.roll(low, q, 1), pltpu.roll(high, q, 1)) if q else (low, high)
            lhs_up[ROWS * i : ROWS * (i + 1), a] = jnp.where(lane < q, 0.0, lo).astype(bf16)
            lhs_up[ROWS * i : ROWS * (i + 1), b] = jnp.where(lane < q, lo, hi).astype(bf16)
        for i in range(DOWN):
            q = 128 - (2 * i + 1)
            lo, hi = pltpu.roll(low, q, 1), pltpu.roll(high, q, 1)
            lhs_down[ROWS * i : ROWS * (i + 1), a] = jnp.where(lane < q, lo, hi).astype(bf16)
            lhs_down[ROWS * i : ROWS * (i + 1), b] = jnp.where(lane < q, hi, 0.0).astype(bf16)

    up = jnp.dot(lhs_up[...], rhs_up[...], preferred_element_type=f32)
    for i in range(UP):
        block = (up[ROWS * i : ROWS * (i + 1)] * SCALE).astype(bf16)
        lag = MAXLAG + 2 * i
        out_ref[lag] = block[:, :CH]
        if lag + 1 < LAGS:
            out_ref[lag + 1] = block[:, CH:]
    down = jnp.dot(lhs_down[...], rhs_down[...], preferred_element_type=f32)
    for i in range(DOWN):
        block = (down[ROWS * i : ROWS * (i + 1)] * SCALE).astype(bf16)
        lag = MAXLAG - 1 - 2 * i
        out_ref[lag] = block[:, :CH]
        out_ref[lag - 1] = block[:, CH:]

    for copy in first + gather + second + third[1:] + [swap]:
        copy.wait_send()
    pl.when(jnp.logical_not(own))(lambda: third[0].wait_send())


def body(raw_strain, fir_taps, source_ids):
    hbm = pl.BlockSpec(memory_space=pltpu.HBM)
    dma = pltpu.SemaphoreType.DMA
    signals = pltpu.SemaphoreType.REGULAR
    out = pl.pallas_call(
        kernel,
        out_shape=jax.ShapeDtypeStruct((LAGS, ROWS, CH), bf16),
        in_specs=[hbm, hbm, hbm],
        out_specs=pl.BlockSpec(memory_space=pltpu.VMEM),
        scratch_shapes=[
            pltpu.VMEM((1, CH, RAW), bf16),
            pltpu.SMEM((NTAP,), f32),
            pltpu.VMEM((4, 32), jnp.int32),
            pltpu.VMEM((SEG, CH, SAMPLES), bf16),
            pltpu.VMEM((SEG, 2, ROWS, 128), bf16),
            pltpu.VMEM((7, 2, ROWS, 128), bf16),
            pltpu.VMEM((2, ROWS, 128), bf16),
            pltpu.VMEM((NYC, ROWS, 128), bf16),
            pltpu.VMEM((ROWS, 128), bf16),
            pltpu.VMEM((2 * SEG, ROWS, 128), bf16),
            pltpu.VMEM((2, SEG, ROWS, 128), bf16),
            pltpu.VMEM((ROWS * UP, SEG * SAMPLES), bf16),
            pltpu.VMEM((ROWS * DOWN, SEG * SAMPLES), bf16),
            pltpu.VMEM((SEG * SAMPLES, 2 * CH), bf16),
            pltpu.VMEM((SEG * SAMPLES, 2 * CH), bf16),
            dma((3,)),
            dma((SEG,)), dma((SEG,)),
            dma((7,)), dma((7,)),
            dma((NYC,)), dma((NYC,)),
            dma((NZ,)), dma((2 * SEG,)),
            dma, dma,
            signals, signals,
        ],
        compiler_params=pltpu.CompilerParams(
            collective_id=0, has_side_effects=True, vmem_limit_bytes=60 * 1024 * 1024
        ),
    )(raw_strain, fir_taps, source_ids)
    return out.transpose(1, 0, 2)


def solution(mesh):
    return jax.shard_map(
        body,
        mesh=mesh,
        in_specs=(P("tm", "array", None), P(), P()),
        out_specs=P("tm", None, "array"),
        check_vma=False,
    )
```

```python
import functools
import math

import jax
import jax.numpy as jnp
from jax import lax
from jax.experimental import pallas as pl
from jax.experimental.pallas import tpu as pltpu
from jax.sharding import PartitionSpec as P

MESH = pl.DeviceIdType.MESH
SOURCES = 128
MAXLAG = 50
WINDOW = 64
DECIM = 4
NTAP = 8
SAMPLES = 256
LAGS = 101
RAW = 1024
SEG = 8
ROWS = 16
CH = 128
NZ = 16
NYC = 4
PLACES = NZ * NYC
SUMS = 16
SIDE = PLACES // 2
UP = 26
DOWN = 25
EPSILON = 1e-05
SCALE = 1.0 / (math.sqrt(SAMPLES) * math.sqrt(SEG))

f32 = jnp.float32
bf16 = jnp.bfloat16
TN = (((0,), (0,)), ((), ()))


def iota(shape, dim):
    return lax.broadcasted_iota(jnp.int32, shape, dim)


def terms(value, count):
    parts = []
    for _ in range(count):
        part = value.astype(bf16)
        parts.append(part)
        value = value - part.astype(f32)
    return parts


def tap_bands(taps_ref):
    k = DECIM * iota((128, 128), 1) - iota((128, 128), 0)
    band = jnp.zeros((128, 128), f32)
    for tap in range(NTAP):
        band = jnp.where(k == tap, taps_ref[tap], band)
    band = jnp.concatenate([band, jnp.zeros((128, 128), f32)], 1)
    lane = iota((128, SAMPLES), 1)
    bands = []
    for tile in range(RAW // 128):
        placed = pltpu.roll(band, 32 * tile, 1) if tile else band
        if tile == RAW // 128 - 1:
            placed = jnp.where(lane < 2, 0.0, placed)
        bands.append(terms(placed, 3))
    return bands


def normalize(raw, bands):
    filtered = jnp.zeros((CH, SAMPLES), f32)
    for term in range(3):
        matrix = jnp.concatenate([band[term] for band in bands], 0)
        filtered = filtered + jnp.dot(raw, matrix, preferred_element_type=f32)
    gap = iota((SAMPLES, SAMPLES), 0) - iota((SAMPLES, SAMPLES), 1)
    window = jnp.where((gap >= -(WINDOW // 2)) & (gap < WINDOW // 2), 1.0, 0.0).astype(bf16)
    total = jnp.zeros((CH, SAMPLES), f32)
    for part in terms(jnp.abs(filtered), 2):
        total = total + jnp.dot(part, window, preferred_element_type=f32)
    return filtered / (total * (1.0 / WINDOW) + EPSILON)


def kernel(
    raw_hbm, taps_hbm, ids_hbm, out_ref,
    raw, taps, ids_ref, xall, send0, recv0, send1, recv1, mine, parts, lhs_up, lhs_down, rhs_up, rhs_down,
    in_sem, x_send, x_recv, s0_send, s0_recv, s1_send, s1_recv, s2_send, s2_recv, s3_send, s3_recv, column, ready,
):
    inputs = [
        pltpu.make_async_copy(src, dst, in_sem.at[i])
        for i, (src, dst) in enumerate(((taps_hbm, taps), (raw_hbm, raw), (ids_hbm, ids_ref)))
    ]
    for copy in inputs:
        copy.start()

    tm = lax.axis_index("tm")
    place = lax.axis_index("array")
    z = lax.div(place, NYC)
    core = lax.rem(place, 2)
    side = lax.rem(lax.div(place, 2), 2)
    other = place + 1 - 2 * core
    sums = place < SUMS
    owner = z + 4 * side

    def along_tm(d):
        return {"tm": lax.rem(tm + d, SEG), "array": place}

    def signal(semaphore, device):
        pl.semaphore_signal(semaphore, inc=1, device_id=device, device_id_type=MESH)

    barrier = pltpu.get_barrier_semaphore()
    for d in range(1, SEG):
        signal(barrier, along_tm(d))
    signal(barrier, {"tm": tm, "array": other})

    @pl.when(sums)
    def _():
        def greet(d, carry):
            signal(barrier, {"tm": tm, "array": lax.rem(place + 2 * d, PLACES)})
            return carry

        lax.fori_loop(1, SIDE, greet, 0)

    inputs[0].wait()
    bands = tap_bands(taps)
    inputs[1].wait()
    normed = normalize(raw[0], bands)
    xall[tm] = normed.astype(bf16)

    inputs[2].wait()
    ids = jnp.concatenate([ids_ref[r : r + 1, :] for r in range(4)], 1)
    chosen = (iota((CH, SOURCES), 0) == ids - place * CH).astype(f32).astype(bf16)
    picked = lax.dot_general(chosen, xall[tm], TN, preferred_element_type=f32)
    for t in range(SEG):
        for h in range(2):
            part = picked[ROWS * t + 8 * h : ROWS * t + 8 * h + 8]
            send0[h, t] = jnp.concatenate([part[:, :128], part[:, 128:]], 0).astype(bf16)

    pl.semaphore_wait(barrier, jnp.where(sums, SEG - 1, SEG) + SEG - 1 + 1)

    halves = pltpu.make_async_remote_copy(
        send0.at[1 - core], recv0, s0_send, s0_recv, {"tm": tm, "array": other}, MESH
    )
    halves.start()

    @pl.when(jnp.logical_not(sums))
    def _():
        for k in range(0, SUMS, 2):
            signal(column, {"tm": tm, "array": k + core})

    halves.wait_recv()
    for t in range(SEG):
        send1[t] = (send0[core, t].astype(f32) + recv0[t].astype(f32)).astype(bf16)

    for i in range(SEG):
        plane = jnp.where(z < 10, i // 2, 3 - i // 2)
        across = lax.rem(side + 1 + i, 2)
        k = plane * NYC + 2 * across + core
        copy = pltpu.make_async_remote_copy(
            send1.at[plane + 4 * across], recv1.at[lax.div(lax.rem(place - k + PLACES, PLACES), 2)],
            s1_send, s1_recv, {"tm": tm, "array": k}, MESH,
        )
        pl.when(place != k)(copy.start)

    gather = [
        pltpu.make_async_remote_copy(
            xall.at[tm], xall.at[tm], x_send.at[d], x_recv.at[d], along_tm(d), MESH
        )
        for d in range(1, SEG)
    ]
    for copy in gather:
        copy.start()

    @pl.when(sums)
    def _():
        pl.semaphore_wait(column, SIDE - SEG)

        @pl.when(tm == owner)
        def _():
            for d in range(1, SEG):
                signal(ready, along_tm(d))

    @pl.when(sums)
    def _():
        others = recv1.at[pl.ds(1, SIDE - 1)]
        pltpu.make_async_copy(others, others, s1_recv).wait()
        total = send1[owner].astype(f32)
        for i in range(1, SIDE):
            total = total + recv1[i].astype(f32)
        mine[...] = total.astype(bf16)
        pl.when(tm != owner)(lambda: pl.semaphore_wait(ready, 1))

        def spread(i, carry):
            p = 2 * i + core
            copy = pltpu.make_async_remote_copy(
                mine, parts.at[core, tm], s2_send, s2_recv, {"tm": owner, "array": p}, MESH
            )
            here = (tm == owner) & (p == place)
            pl.when(jnp.logical_not(here))(copy.start)
            return carry

        lax.fori_loop(0, SIDE, spread, 0)
        pl.when(tm == owner)(lambda: pltpu.make_async_copy(mine, parts.at[core, tm], s2_recv).start())

    step = iota((SAMPLES, CH), 0)
    for copy in gather:
        copy.wait_recv()
    for g in range(SEG):
        x = xall[g].astype(f32).T
        later = jnp.where(step == SAMPLES - 1, 0.0, pltpu.roll(x, SAMPLES - 1, 0))
        earlier = jnp.where(step == 0, 0.0, pltpu.roll(x, 1, 0))
        span = slice(SAMPLES * g, SAMPLES * (g + 1))
        rhs_up[span, :CH] = x.astype(bf16)
        rhs_up[span, CH:] = later.astype(bf16)
        rhs_down[span, :CH] = x.astype(bf16)
        rhs_down[span, CH:] = earlier.astype(bf16)

    pltpu.make_async_copy(parts.at[core], parts.at[core], s2_recv).wait()

    swap = pltpu.make_async_remote_copy(
        parts.at[core], parts.at[core], s3_send, s3_recv, {"tm": tm, "array": other}, MESH
    )
    swap.start()
    swap.wait_recv()

    lane = iota((ROWS, 128), 1)
    for g in range(SEG):
        one = parts[0, g].astype(f32)
        two = parts[1, g].astype(f32)
        low = jnp.concatenate([one[:8], two[:8]], 0)
        high = jnp.concatenate([one[8:], two[8:]], 0)
        a, b = slice(256 * g, 256 * g + 128), slice(256 * g + 128, 256 * g + 256)
        for i in range(UP):
            q = 2 * i
            lo, hi = (pltpu.roll(low, q, 1), pltpu.roll(high, q, 1)) if q else (low, high)
            lhs_up[ROWS * i : ROWS * (i + 1), a] = jnp.where(lane < q, 0.0, lo).astype(bf16)
            lhs_up[ROWS * i : ROWS * (i + 1), b] = jnp.where(lane < q, lo, hi).astype(bf16)
        for i in range(DOWN):
            q = 128 - (2 * i + 1)
            lo, hi = pltpu.roll(low, q, 1), pltpu.roll(high, q, 1)
            lhs_down[ROWS * i : ROWS * (i + 1), a] = jnp.where(lane < q, lo, hi).astype(bf16)
            lhs_down[ROWS * i : ROWS * (i + 1), b] = jnp.where(lane < q, hi, 0.0).astype(bf16)

    up = jnp.dot(lhs_up[...], rhs_up[...], preferred_element_type=f32)
    for i in range(UP):
        block = (up[ROWS * i : ROWS * (i + 1)] * SCALE).astype(bf16)
        lag = MAXLAG + 2 * i
        out_ref[lag] = block[:, :CH]
        if lag + 1 < LAGS:
            out_ref[lag + 1] = block[:, CH:]
    down = jnp.dot(lhs_down[...], rhs_down[...], preferred_element_type=f32)
    for i in range(DOWN):
        block = (down[ROWS * i : ROWS * (i + 1)] * SCALE).astype(bf16)
        lag = MAXLAG - 1 - 2 * i
        out_ref[lag] = block[:, :CH]
        out_ref[lag - 1] = block[:, CH:]

    for copy in gather + [halves, swap]:
        copy.wait_send()

    @pl.when(jnp.logical_not(sums))
    def _():
        pltpu.make_async_copy(send1, send1, s1_send).wait()

    @pl.when(sums)
    def _():
        fewer = send1.at[pl.ds(1, SEG - 1)]
        pltpu.make_async_copy(fewer, fewer, s1_send).wait()
        others = recv1.at[pl.ds(1, SIDE - 1)]
        pl.when(tm != owner)(lambda: pltpu.make_async_copy(recv1, recv1, s2_send).wait())
        pl.when(tm == owner)(lambda: pltpu.make_async_copy(others, others, s2_send).wait())


def body(raw_strain, fir_taps, source_ids):
    hbm = pl.BlockSpec(memory_space=pltpu.HBM)
    dma = pltpu.SemaphoreType.DMA
    signals = pltpu.SemaphoreType.REGULAR
    out = pl.pallas_call(
        kernel,
        out_shape=jax.ShapeDtypeStruct((LAGS, ROWS, CH), bf16),
        in_specs=[hbm, hbm, hbm],
        out_specs=pl.BlockSpec(memory_space=pltpu.VMEM),
        scratch_shapes=[
            pltpu.VMEM((1, CH, RAW), bf16),
            pltpu.SMEM((NTAP,), f32),
            pltpu.VMEM((4, 32), jnp.int32),
            pltpu.VMEM((SEG, CH, SAMPLES), bf16),
            pltpu.VMEM((2, SEG, 16, 128), bf16),
            pltpu.VMEM((SEG, 16, 128), bf16),
            pltpu.VMEM((SEG, 16, 128), bf16),
            pltpu.VMEM((SIDE, 16, 128), bf16),
            pltpu.VMEM((16, 128), bf16),
            pltpu.VMEM((2, SEG, 16, 128), bf16),
            pltpu.VMEM((ROWS * UP, SEG * SAMPLES), bf16),
            pltpu.VMEM((ROWS * DOWN, SEG * SAMPLES), bf16),
            pltpu.VMEM((SEG * SAMPLES, 2 * CH), bf16),
            pltpu.VMEM((SEG * SAMPLES, 2 * CH), bf16),
            dma((3,)),
            dma((SEG,)), dma((SEG,)),
            dma, dma,
            dma, dma,
            dma, dma,
            dma, dma,
            signals, signals,
        ],
        compiler_params=pltpu.CompilerParams(
            collective_id=0, has_side_effects=True, vmem_limit_bytes=60 * 1024 * 1024
        ),
    )(raw_strain, fir_taps, source_ids)
    return out.transpose(1, 0, 2)


def solution(mesh):
    return jax.shard_map(
        body,
        mesh=mesh,
        in_specs=(P("tm", "array", None), P(), P()),
        out_specs=P("tm", None, "array"),
        check_vma=False,
    )
```

```python
import functools
import math

import jax
import jax.numpy as jnp
from jax import lax
from jax.experimental import pallas as pl
from jax.experimental.pallas import tpu as pltpu
from jax.sharding import PartitionSpec as P

MESH = pl.DeviceIdType.MESH
SOURCES = 128
MAXLAG = 50
WINDOW = 64
DECIM = 4
NTAP = 8
SAMPLES = 256
LAGS = 101
RAW = 1024
SEG = 8
ROWS = 16
CH = 128
NZ = 16
NYC = 4
PLACES = NZ * NYC
SUMS = 16
SIDE = PLACES // 2
USERS = SUMS + (PLACES - SUMS) // 2
UP = 26
DOWN = 25
EPSILON = 1e-05
SCALE = 1.0 / (math.sqrt(SAMPLES) * math.sqrt(SEG))

f32 = jnp.float32
bf16 = jnp.bfloat16
TN = (((0,), (0,)), ((), ()))


def iota(shape, dim):
    return lax.broadcasted_iota(jnp.int32, shape, dim)


def terms(value, count):
    parts = []
    for _ in range(count):
        part = value.astype(bf16)
        parts.append(part)
        value = value - part.astype(f32)
    return parts


def tap_bands(taps_ref):
    k = DECIM * iota((128, 128), 1) - iota((128, 128), 0)
    band = jnp.zeros((128, 128), f32)
    for tap in range(NTAP):
        band = jnp.where(k == tap, taps_ref[tap], band)
    band = jnp.concatenate([band, jnp.zeros((128, 128), f32)], 1)
    lane = iota((128, SAMPLES), 1)
    bands = []
    for tile in range(RAW // 128):
        placed = pltpu.roll(band, 32 * tile, 1) if tile else band
        if tile == RAW // 128 - 1:
            placed = jnp.where(lane < 2, 0.0, placed)
        bands.append(terms(placed, 3))
    return bands


def normalize(raw, bands):
    filtered = jnp.zeros((CH, SAMPLES), f32)
    for term in range(3):
        matrix = jnp.concatenate([band[term] for band in bands], 0)
        filtered = filtered + jnp.dot(raw, matrix, preferred_element_type=f32)
    gap = iota((SAMPLES, SAMPLES), 0) - iota((SAMPLES, SAMPLES), 1)
    window = jnp.where((gap >= -(WINDOW // 2)) & (gap < WINDOW // 2), 1.0, 0.0).astype(bf16)
    total = jnp.zeros((CH, SAMPLES), f32)
    for part in terms(jnp.abs(filtered), 2):
        total = total + jnp.dot(part, window, preferred_element_type=f32)
    return filtered / (total * (1.0 / WINDOW) + EPSILON)


def kernel(
    raw_hbm, taps_hbm, ids_hbm, out_ref,
    raw, taps, ids_ref, xall, send0, recv0, send1, recv1, mine, parts, lhs_up, lhs_down, rhs_up, rhs_down,
    in_sem, x_send, x_recv, s0_send, s0_recv, s1_send, s1_recv, s2_send, s2_recv, s3_send, s3_recv, column, beside, beyond, ready,
):
    inputs = [
        pltpu.make_async_copy(src, dst, in_sem.at[i])
        for i, (src, dst) in enumerate(((taps_hbm, taps), (raw_hbm, raw), (ids_hbm, ids_ref)))
    ]
    for copy in inputs:
        copy.start()

    tm = lax.axis_index("tm")
    place = lax.axis_index("array")
    z = lax.div(place, NYC)
    core = lax.rem(place, 2)
    side = lax.rem(lax.div(place, 2), 2)
    other = place + 1 - 2 * core
    sums = place < SUMS
    owner = z + 4 * side

    right, left = lax.rem(tm + 2, SEG), lax.rem(tm + 6, SEG)
    across = tm + 1 - 2 * lax.rem(tm, 2)

    def in_tm(t):
        return {"tm": t, "array": place}

    def signal(semaphore, device):
        pl.semaphore_signal(semaphore, inc=1, device_id=device, device_id_type=MESH)

    barrier = pltpu.get_barrier_semaphore()
    for t in (across, left, right):
        signal(barrier, in_tm(t))
    pl.when(jnp.logical_not(sums))(lambda: signal(barrier, {"tm": tm, "array": other}))

    @pl.when(sums)
    def _():
        def greet(d, carry):
            signal(barrier, {"tm": tm, "array": lax.rem(place + 2 * d, PLACES)})
            return carry

        for k in range(0, SUMS, 2):
            signal(barrier, {"tm": tm, "array": k + 1 - core})
        lax.fori_loop(1, SIDE, greet, 0)

    inputs[0].wait()
    bands = tap_bands(taps)

    pl.semaphore_wait(barrier, jnp.where(sums, SUMS - 1, SEG + 1) + 3)

    @pl.when(jnp.logical_not(sums))
    def _():
        for k in range(0, SUMS, 2):
            signal(column, {"tm": tm, "array": k + core})

    signal(beside, in_tm(left))
    signal(beside, in_tm(across))

    inputs[1].wait()
    normed = normalize(raw[0], bands)
    xall[tm] = normed.astype(bf16)

    inputs[2].wait()
    ids = jnp.concatenate([ids_ref[r : r + 1, :] for r in range(4)], 1)
    chosen = (iota((CH, SOURCES), 0) == ids - place * CH).astype(f32).astype(bf16)
    picked = lax.dot_general(chosen, xall[tm], TN, preferred_element_type=f32)
    for t in range(SEG):
        for h in range(2):
            part = picked[ROWS * t + 8 * h : ROWS * t + 8 * h + 8]
            send0[h, t] = jnp.concatenate([part[:, :128], part[:, 128:]], 0).astype(bf16)

    halves = pltpu.make_async_remote_copy(
        send0.at[1 - core], recv0, s0_send, s0_recv, {"tm": tm, "array": other}, MESH
    )
    halves.start()

    pl.semaphore_wait(beside, 2)
    signal(beyond, in_tm(across))


    halves.wait_recv()
    for t in range(SEG):
        send1[t] = (send0[core, t].astype(f32) + recv0[t].astype(f32)).astype(bf16)

    for i in range(SEG):
        plane = jnp.where(z < 10, i // 2, 3 - i // 2)
        to_side = lax.rem(side + 1 + i, 2)
        k = plane * NYC + 2 * to_side + core
        copy = pltpu.make_async_remote_copy(
            send1.at[plane + 4 * to_side], recv1.at[lax.div(lax.rem(place - k + PLACES, PLACES), 2)],
            s1_send, s1_recv, {"tm": tm, "array": k}, MESH,
        )
        pl.when(place != k)(copy.start)

    pl.semaphore_wait(beyond, 1)
    gather = [
        pltpu.make_async_remote_copy(
            xall.at[tm], xall.at[tm], x_send.at[d], x_recv.at[d], in_tm(lax.rem(tm + d, SEG)), MESH
        )
        for d in range(1, SEG)
    ]
    for copy in gather:
        copy.start()

    @pl.when(sums)
    def _():
        pl.semaphore_wait(column, SIDE - SEG)

        @pl.when(tm == owner)
        def _():
            for d in range(1, SEG):
                signal(ready, in_tm(lax.rem(tm + d, SEG)))

    @pl.when(sums)
    def _():
        others = recv1.at[pl.ds(1, SIDE - 1)]
        pltpu.make_async_copy(others, others, s1_recv).wait()
        total = send1[owner].astype(f32)
        for i in range(1, SIDE):
            total = total + recv1[i].astype(f32)
        mine[...] = total.astype(bf16)
        pl.when(tm != owner)(lambda: pl.semaphore_wait(ready, 1))

        def spread(i, carry):
            p = jnp.where(i < SUMS, i, 2 * i - SUMS + core)
            copy = pltpu.make_async_remote_copy(
                mine, parts.at[core, tm], s2_send, s2_recv, {"tm": owner, "array": p}, MESH
            )
            here = (tm == owner) & (p == place)
            pl.when(jnp.logical_not(here))(copy.start)
            return carry

        lax.fori_loop(0, USERS, spread, 0)
        pl.when(tm == owner)(lambda: pltpu.make_async_copy(mine, parts.at[core, tm], s2_recv).start())

    step = iota((SAMPLES, CH), 0)
    for copy in gather:
        copy.wait_recv()
    for g in range(SEG):
        x = xall[g].astype(f32).T
        later = jnp.where(step == SAMPLES - 1, 0.0, pltpu.roll(x, SAMPLES - 1, 0))
        earlier = jnp.where(step == 0, 0.0, pltpu.roll(x, 1, 0))
        span = slice(SAMPLES * g, SAMPLES * (g + 1))
        rhs_up[span, :CH] = x.astype(bf16)
        rhs_up[span, CH:] = later.astype(bf16)
        rhs_down[span, :CH] = x.astype(bf16)
        rhs_down[span, CH:] = earlier.astype(bf16)

    swap = pltpu.make_async_remote_copy(
        parts.at[core], parts.at[core], s3_send, s3_recv, {"tm": tm, "array": other}, MESH
    )
    pl.when(sums)(lambda: pltpu.make_async_copy(parts, parts, s2_recv).wait())

    @pl.when(jnp.logical_not(sums))
    def _():
        pltpu.make_async_copy(parts.at[core], parts.at[core], s2_recv).wait()
        swap.start()
        swap.wait_recv()

    lane = iota((ROWS, 128), 1)
    for g in range(SEG):
        one = parts[0, g].astype(f32)
        two = parts[1, g].astype(f32)
        low = jnp.concatenate([one[:8], two[:8]], 0)
        high = jnp.concatenate([one[8:], two[8:]], 0)
        a, b = slice(256 * g, 256 * g + 128), slice(256 * g + 128, 256 * g + 256)
        for i in range(UP):
            q = 2 * i
            lo, hi = (pltpu.roll(low, q, 1), pltpu.roll(high, q, 1)) if q else (low, high)
            lhs_up[ROWS * i : ROWS * (i + 1), a] = jnp.where(lane < q, 0.0, lo).astype(bf16)
            lhs_up[ROWS * i : ROWS * (i + 1), b] = jnp.where(lane < q, lo, hi).astype(bf16)
        for i in range(DOWN):
            q = 128 - (2 * i + 1)
            lo, hi = pltpu.roll(low, q, 1), pltpu.roll(high, q, 1)
            lhs_down[ROWS * i : ROWS * (i + 1), a] = jnp.where(lane < q, lo, hi).astype(bf16)
            lhs_down[ROWS * i : ROWS * (i + 1), b] = jnp.where(lane < q, hi, 0.0).astype(bf16)

    up = jnp.dot(lhs_up[...], rhs_up[...], preferred_element_type=f32)
    for i in range(UP):
        block = (up[ROWS * i : ROWS * (i + 1)] * SCALE).astype(bf16)
        lag = MAXLAG + 2 * i
        out_ref[lag] = block[:, :CH]
        if lag + 1 < LAGS:
            out_ref[lag + 1] = block[:, CH:]
    down = jnp.dot(lhs_down[...], rhs_down[...], preferred_element_type=f32)
    for i in range(DOWN):
        block = (down[ROWS * i : ROWS * (i + 1)] * SCALE).astype(bf16)
        lag = MAXLAG - 1 - 2 * i
        out_ref[lag] = block[:, :CH]
        out_ref[lag - 1] = block[:, CH:]

    for copy in gather + [halves]:
        copy.wait_send()

    @pl.when(jnp.logical_not(sums))
    def _():
        swap.wait_send()
        pltpu.make_async_copy(send1, send1, s1_send).wait()

    @pl.when(sums)
    def _():
        fewer = send1.at[pl.ds(1, SEG - 1)]
        pltpu.make_async_copy(fewer, fewer, s1_send).wait()
        others = recv1.at[pl.ds(1, USERS - 1)]
        pl.when(tm != owner)(lambda: pltpu.make_async_copy(recv1, recv1, s2_send).wait())
        pl.when(tm == owner)(lambda: pltpu.make_async_copy(others, others, s2_send).wait())


def body(raw_strain, fir_taps, source_ids):
    hbm = pl.BlockSpec(memory_space=pltpu.HBM)
    dma = pltpu.SemaphoreType.DMA
    signals = pltpu.SemaphoreType.REGULAR
    out = pl.pallas_call(
        kernel,
        out_shape=pltpu.VMEM((LAGS, ROWS, CH), bf16),
        in_specs=[hbm, hbm, hbm],
        out_specs=pl.BlockSpec(memory_space=pltpu.VMEM),
        scratch_shapes=[
            pltpu.VMEM((1, CH, RAW), bf16),
            pltpu.SMEM((NTAP,), f32),
            pltpu.VMEM((4, 32), jnp.int32),
            pltpu.VMEM((SEG, CH, SAMPLES), bf16),
            pltpu.VMEM((2, SEG, 16, 128), bf16),
            pltpu.VMEM((SEG, 16, 128), bf16),
            pltpu.VMEM((SEG, 16, 128), bf16),
            pltpu.VMEM((USERS, 16, 128), bf16),
            pltpu.VMEM((16, 128), bf16),
            pltpu.VMEM((2, SEG, 16, 128), bf16),
            pltpu.VMEM((ROWS * UP, SEG * SAMPLES), bf16),
            pltpu.VMEM((ROWS * DOWN, SEG * SAMPLES), bf16),
            pltpu.VMEM((SEG * SAMPLES, 2 * CH), bf16),
            pltpu.VMEM((SEG * SAMPLES, 2 * CH), bf16),
            dma((3,)),
            dma((SEG,)), dma((SEG,)),
            dma, dma,
            dma, dma,
            dma, dma,
            dma, dma,
            signals, signals, signals, signals,
        ],
        compiler_params=pltpu.CompilerParams(
            collective_id=0, has_side_effects=True, vmem_limit_bytes=56 * 1024 * 1024
        ),
    )(raw_strain, fir_taps, source_ids)
    return out.transpose(1, 0, 2)


def solution(mesh):
    return jax.shard_map(
        body,
        mesh=mesh,
        in_specs=(P("tm", "array", None), P(), P()),
        out_specs=P("tm", None, "array"),
        check_vma=False,
    )
```

```python
import functools
import math

import jax
import jax.numpy as jnp
from jax import lax
from jax.experimental import pallas as pl
from jax.experimental.pallas import tpu as pltpu
from jax.sharding import PartitionSpec as P

MESH = pl.DeviceIdType.MESH
SOURCES = 128
MAXLAG = 50
WINDOW = 64
DECIM = 4
NTAP = 8
SAMPLES = 256
LAGS = 101
RAW = 1024
SEG = 8
ROWS = 16
CH = 128
NZ = 16
NYC = 4
PLACES = NZ * NYC
SUMS = 16
SIDE = PLACES // 2
AWAIT = {0: 4, 4: 8}
USERS = SUMS + (PLACES - SUMS) // 2
UP = 26
DOWN = 25
EPSILON = 1e-05
SCALE = 1.0 / (math.sqrt(SAMPLES) * math.sqrt(SEG))

f32 = jnp.float32
bf16 = jnp.bfloat16
TN = (((0,), (0,)), ((), ()))


def iota(shape, dim):
    return lax.broadcasted_iota(jnp.int32, shape, dim)


def terms(value, count):
    parts = []
    for _ in range(count):
        part = value.astype(bf16)
        parts.append(part)
        value = value - part.astype(f32)
    return parts


def tap_bands(taps_ref):
    k = DECIM * iota((128, 128), 1) - iota((128, 128), 0)
    band = jnp.zeros((128, 128), f32)
    for tap in range(NTAP):
        band = jnp.where(k == tap, taps_ref[tap], band)
    band = jnp.concatenate([band, jnp.zeros((128, 128), f32)], 1)
    lane = iota((128, SAMPLES), 1)
    bands = []
    for tile in range(RAW // 128):
        placed = pltpu.roll(band, 32 * tile, 1) if tile else band
        if tile == RAW // 128 - 1:
            placed = jnp.where(lane < 2, 0.0, placed)
        bands.append(terms(placed, 3))
    return bands


def decimate(raw, bands):
    filtered = jnp.zeros((CH, SAMPLES), f32)
    for term in range(3):
        matrix = jnp.concatenate([band[term] for band in bands], 0)
        filtered = filtered + jnp.dot(raw, matrix, preferred_element_type=f32)
    return filtered


def normalize(filtered):
    gap = iota((SAMPLES, SAMPLES), 0) - iota((SAMPLES, SAMPLES), 1)
    window = jnp.where((gap >= -(WINDOW // 2)) & (gap < WINDOW // 2), 1.0, 0.0).astype(bf16)
    total = jnp.zeros((CH, SAMPLES), f32)
    for part in terms(jnp.abs(filtered), 2):
        total = total + jnp.dot(part, window, preferred_element_type=f32)
    return filtered / (total * (1.0 / WINDOW) + EPSILON)


def kernel(
    raw_hbm, taps_hbm, ids_hbm, out_ref,
    raw, taps, ids_ref, xall, send0, recv0, send1, recv1, mine, parts, rhs_up, rhs_down,
    in_sem, x_send, x_recv, s0_send, s0_recv, s1_send, s1_recv, s2_send, s2_recv, s3_send, s3_recv, column, beside, beyond, ready, complete,
):
    inputs = [
        pltpu.make_async_copy(src, dst, in_sem.at[i])
        for i, (src, dst) in enumerate(((taps_hbm, taps), (raw_hbm, raw), (ids_hbm, ids_ref)))
    ]
    for copy in inputs:
        copy.start()

    tm = lax.axis_index("tm")
    place = lax.axis_index("array")
    z = lax.div(place, NYC)
    core = lax.rem(place, 2)
    side = lax.rem(lax.div(place, 2), 2)
    other = place + 1 - 2 * core
    sums = place < SUMS
    owner = z + 4 * side

    right, left = lax.rem(tm + 2, SEG), lax.rem(tm + 6, SEG)
    across = tm + 1 - 2 * lax.rem(tm, 2)

    def in_tm(t):
        return {"tm": t, "array": place}

    def signal(semaphore, device):
        pl.semaphore_signal(semaphore, inc=1, device_id=device, device_id_type=MESH)

    barrier = pltpu.get_barrier_semaphore()
    for t in (across, left, right):
        signal(barrier, in_tm(t))
    pl.when(jnp.logical_not(sums))(lambda: signal(barrier, {"tm": tm, "array": other}))

    @pl.when(sums)
    def _():
        def greet(d, carry):
            signal(barrier, {"tm": tm, "array": lax.rem(place + 2 * d, PLACES)})
            return carry

        for k in range(0, SUMS, 2):
            signal(barrier, {"tm": tm, "array": k + 1 - core})
        lax.fori_loop(1, SIDE, greet, 0)

    inputs[0].wait()
    bands = tap_bands(taps)

    inputs[1].wait()
    filtered = decimate(raw[0], bands)

    pl.semaphore_wait(barrier, jnp.where(sums, SUMS - 1, SEG + 1) + 3)

    @pl.when(jnp.logical_not(sums))
    def _():
        for k in range(0, SUMS, 2):
            signal(column, {"tm": tm, "array": k + core})

    signal(beside, in_tm(left))
    signal(beside, in_tm(across))

    xall[tm] = normalize(filtered).astype(bf16)

    inputs[2].wait()
    ids = jnp.concatenate([ids_ref[r : r + 1, :] for r in range(4)], 1)
    chosen = (iota((CH, SOURCES), 0) == ids - place * CH).astype(f32).astype(bf16)
    picked = lax.dot_general(chosen, xall[tm], TN, preferred_element_type=f32)
    for t in range(SEG):
        for h in range(2):
            part = picked[ROWS * t + 8 * h : ROWS * t + 8 * h + 8]
            send0[h, t] = jnp.concatenate([part[:, :128], part[:, 128:]], 0).astype(bf16)

    halves = pltpu.make_async_remote_copy(
        send0.at[1 - core], recv0, s0_send, s0_recv, {"tm": tm, "array": other}, MESH
    )
    halves.start()

    pl.semaphore_wait(beside, 2)
    signal(beyond, in_tm(across))


    halves.wait_recv()
    for t in range(SEG):
        send1[t] = (send0[core, t].astype(f32) + recv0[t].astype(f32)).astype(bf16)

    for i in range(SEG):
        plane = jnp.where(z < 10, i // 2, 3 - i // 2)
        to_side = lax.rem(side + 1 + i, 2)
        k = plane * NYC + 2 * to_side + core
        copy = pltpu.make_async_remote_copy(
            send1.at[plane + 4 * to_side], recv1.at[lax.div(lax.rem(place - k + PLACES, PLACES), 2)],
            s1_send, s1_recv, {"tm": tm, "array": k}, MESH,
        )
        pl.when(place != k)(copy.start)

    pl.semaphore_wait(beyond, 1)
    gather = [
        pltpu.make_async_remote_copy(
            xall.at[tm], xall.at[tm], x_send.at[d], x_recv.at[d], in_tm(lax.rem(tm + d, SEG)), MESH
        )
        for d in range(1, SEG)
    ]
    for copy in gather:
        copy.start()

    def announce(semaphore):
        for d in range(1, SEG):
            signal(semaphore, in_tm(lax.rem(tm + d, SEG)))

    @pl.when(sums)
    def _():
        pl.when(tm == owner)(lambda: announce(ready))
        pl.semaphore_wait(column, SIDE - SEG)
        pl.when(tm == owner)(lambda: announce(complete))

    @pl.when(sums)
    def _():
        others = recv1.at[pl.ds(1, SIDE - 1)]
        pltpu.make_async_copy(others, others, s1_recv).wait()
        total = send1[owner].astype(f32)
        for i in range(1, SIDE):
            total = total + recv1[i].astype(f32)
        mine[...] = total.astype(bf16)
        pl.when(tm != owner)(lambda: pl.semaphore_wait(ready, 1))

        def spread(p):
            copy = pltpu.make_async_remote_copy(
                mine, parts.at[core, tm], s2_send, s2_recv.at[tm], {"tm": owner, "array": p}, MESH
            )
            pl.when(jnp.logical_not((tm == owner) & (p == place)))(copy.start)

        for p in range(0, SUMS, 2):
            spread(p + 1)
            spread(p)
        pl.when(tm != owner)(lambda: pl.semaphore_wait(complete, 1))

        def one_side(i, carry):
            spread(2 * i + core)
            return carry

        lax.fori_loop(SUMS // 2, SIDE, one_side, 0)
        pl.when(tm == owner)(lambda: pltpu.make_async_copy(mine, parts.at[core, tm], s2_recv.at[tm]).start())

    step = iota((SAMPLES, CH), 0)
    for copy in gather:
        copy.wait_recv()
    for g in range(SEG):
        x = xall[g].astype(f32).T
        later = jnp.where(step == SAMPLES - 1, 0.0, pltpu.roll(x, SAMPLES - 1, 0))
        earlier = jnp.where(step == 0, 0.0, pltpu.roll(x, 1, 0))
        rhs_up[g, :, :CH] = x.astype(bf16)
        rhs_up[g, :, CH:] = later.astype(bf16)
        rhs_down[g, :, :CH] = x.astype(bf16)
        rhs_down[g, :, CH:] = earlier.astype(bf16)

    swap = pltpu.make_async_remote_copy(
        parts.at[core], parts.at[core], s3_send, s3_recv, {"tm": tm, "array": other}, MESH
    )

    @pl.when(jnp.logical_not(sums))
    def _():
        for g in range(SEG):
            pltpu.make_async_copy(mine, mine, s2_recv.at[g]).wait()
        swap.start()
        swap.wait_recv()

    lane = iota((ROWS, 128), 1)
    none = jnp.zeros((ROWS, 128), bf16)
    rising = jnp.zeros((ROWS * UP, 2 * CH), f32)
    falling = jnp.zeros((ROWS * DOWN, 2 * CH), f32)
    order = [lax.rem(g, SEG) for g in (tm, right, left, across, tm + 4, across + 2, across + 6, across + 4)]
    pair = send1.at[pl.ds(0, 2)]
    for i, g in enumerate(order):
        if i in AWAIT:

            @pl.when(sums)
            def _():
                for j in range(i, AWAIT[i]):
                    pltpu.make_async_copy(pair, pair, s2_recv.at[order[j]]).wait()

        one = parts[0, g].astype(f32)
        two = parts[1, g].astype(f32)
        low = jnp.concatenate([one[:8], two[:8]], 0).astype(bf16)
        high = jnp.concatenate([one[8:], two[8:]], 0).astype(bf16)
        later, earlier = [], []
        for i in range(UP):
            q = 2 * i
            lo, hi = (pltpu.roll(low, q, 1), pltpu.roll(high, q, 1)) if q else (low, high)
            later.append(jnp.concatenate([jnp.where(lane < q, none, lo), jnp.where(lane < q, lo, hi)], 1))
        for i in range(DOWN):
            q = 128 - (2 * i + 1)
            lo, hi = pltpu.roll(low, q, 1), pltpu.roll(high, q, 1)
            earlier.append(jnp.concatenate([jnp.where(lane < q, lo, hi), jnp.where(lane < q, hi, none)], 1))
        rising = rising + jnp.dot(jnp.concatenate(later, 0), rhs_up[g], preferred_element_type=f32)
        falling = falling + jnp.dot(jnp.concatenate(earlier, 0), rhs_down[g], preferred_element_type=f32)

    for i in range(UP):
        block = (rising[ROWS * i : ROWS * (i + 1)] * SCALE).astype(bf16)
        lag = MAXLAG + 2 * i
        out_ref[lag] = block[:, :CH]
        if lag + 1 < LAGS:
            out_ref[lag + 1] = block[:, CH:]
    for i in range(DOWN):
        block = (falling[ROWS * i : ROWS * (i + 1)] * SCALE).astype(bf16)
        lag = MAXLAG - 1 - 2 * i
        out_ref[lag] = block[:, :CH]
        out_ref[lag - 1] = block[:, CH:]

    for copy in gather + [halves]:
        copy.wait_send()

    pl.when(jnp.logical_not(sums))(swap.wait_send)

    @pl.when(jnp.logical_not(sums))
    def _():
        pltpu.make_async_copy(send1, send1, s1_send).wait()

    @pl.when(sums)
    def _():
        fewer = send1.at[pl.ds(1, SEG - 1)]
        pltpu.make_async_copy(fewer, fewer, s1_send).wait()
        others = recv1.at[pl.ds(1, USERS - 1)]
        pl.when(tm != owner)(lambda: pltpu.make_async_copy(recv1, recv1, s2_send).wait())
        pl.when(tm == owner)(lambda: pltpu.make_async_copy(others, others, s2_send).wait())


def body(raw_strain, fir_taps, source_ids):
    hbm = pl.BlockSpec(memory_space=pltpu.HBM)
    dma = pltpu.SemaphoreType.DMA
    signals = pltpu.SemaphoreType.REGULAR
    out = pl.pallas_call(
        kernel,
        out_shape=pltpu.VMEM((LAGS, ROWS, CH), bf16),
        in_specs=[hbm, hbm, hbm],
        out_specs=pl.BlockSpec(memory_space=pltpu.VMEM),
        scratch_shapes=[
            pltpu.VMEM((1, CH, RAW), bf16),
            pltpu.SMEM((NTAP,), f32),
            pltpu.VMEM((4, 32), jnp.int32),
            pltpu.VMEM((SEG, CH, SAMPLES), bf16),
            pltpu.VMEM((2, SEG, 16, 128), bf16),
            pltpu.VMEM((SEG, 16, 128), bf16),
            pltpu.VMEM((SEG, 16, 128), bf16),
            pltpu.VMEM((USERS, 16, 128), bf16),
            pltpu.VMEM((16, 128), bf16),
            pltpu.VMEM((2, SEG, 16, 128), bf16),
            pltpu.VMEM((SEG, SAMPLES, 2 * CH), bf16),
            pltpu.VMEM((SEG, SAMPLES, 2 * CH), bf16),
            dma((3,)),
            dma((SEG,)), dma((SEG,)),
            dma, dma,
            dma, dma,
            dma, dma((SEG,)),
            dma, dma,
            signals, signals, signals, signals, signals,
        ],
        compiler_params=pltpu.CompilerParams(
            collective_id=0, has_side_effects=True, vmem_limit_bytes=56 * 1024 * 1024
        ),
    )(raw_strain, fir_taps, source_ids)
    return out.transpose(1, 0, 2)


def solution(mesh):
    return jax.shard_map(
        body,
        mesh=mesh,
        in_specs=(P("tm", "array", None), P(), P()),
        out_specs=P("tm", None, "array"),
        check_vma=False,
    )
```

```python
import functools
import math

import jax
import jax.numpy as jnp
from jax import lax
from jax.experimental import pallas as pl
from jax.experimental.pallas import tpu as pltpu
from jax.sharding import PartitionSpec as P

MESH = pl.DeviceIdType.MESH
SOURCES = 128
MAXLAG = 50
WINDOW = 64
DECIM = 4
NTAP = 8
SAMPLES = 256
LAGS = 101
RAW = 1024
SEG = 8
ROWS = 16
CH = 128
NZ = 16
NYC = 4
PLACES = NZ * NYC
SUMS = 16
SIDE = PLACES // 2
AWAIT = {0: 4, 4: 8}
USERS = SUMS + (PLACES - SUMS) // 2
UP = 26
DOWN = 25
EPSILON = 1e-05
SCALE = 1.0 / (math.sqrt(SAMPLES) * math.sqrt(SEG))

f32 = jnp.float32
bf16 = jnp.bfloat16
TN = (((0,), (0,)), ((), ()))


def iota(shape, dim):
    return lax.broadcasted_iota(jnp.int32, shape, dim)


def terms(value, count):
    parts = []
    for _ in range(count):
        part = value.astype(bf16)
        parts.append(part)
        value = value - part.astype(f32)
    return parts


def tap_bands(taps_ref):
    k = DECIM * iota((128, 128), 1) - iota((128, 128), 0)
    band = jnp.zeros((128, 128), f32)
    for tap in range(NTAP):
        band = jnp.where(k == tap, taps_ref[tap], band)
    band = jnp.concatenate([band, jnp.zeros((128, 128), f32)], 1)
    lane = iota((128, SAMPLES), 1)
    bands = []
    for tile in range(RAW // 128):
        placed = pltpu.roll(band, 32 * tile, 1) if tile else band
        if tile == RAW // 128 - 1:
            placed = jnp.where(lane < 2, 0.0, placed)
        bands.append(terms(placed, 3))
    return bands


def decimate(raw, bands):
    filtered = jnp.zeros((CH, SAMPLES), f32)
    for term in range(3):
        matrix = jnp.concatenate([band[term] for band in bands], 0)
        filtered = filtered + jnp.dot(raw, matrix, preferred_element_type=f32)
    return filtered


def normalize(filtered):
    gap = iota((SAMPLES, SAMPLES), 0) - iota((SAMPLES, SAMPLES), 1)
    window = jnp.where((gap >= -(WINDOW // 2)) & (gap < WINDOW // 2), 1.0, 0.0).astype(bf16)
    total = jnp.zeros((CH, SAMPLES), f32)
    for part in terms(jnp.abs(filtered), 2):
        total = total + jnp.dot(part, window, preferred_element_type=f32)
    return filtered / (total * (1.0 / WINDOW) + EPSILON)


def kernel(
    raw_hbm, taps_hbm, ids_hbm, out_ref,
    raw, taps, ids_ref, xall, send0, recv0, send1, recv1, mine, parts, rhs_up, rhs_down,
    in_sem, x_send, x_recv, s0_send, s0_recv, s1_send, s1_recv, s2_send, s2_recv, s3_send, s3_recv, column, beside, beyond, ready, complete,
):
    inputs = [
        pltpu.make_async_copy(src, dst, in_sem.at[i])
        for i, (src, dst) in enumerate(((taps_hbm, taps), (raw_hbm, raw), (ids_hbm, ids_ref)))
    ]
    for copy in inputs:
        copy.start()

    tm = lax.axis_index("tm")
    place = lax.axis_index("array")
    z = lax.div(place, NYC)
    core = lax.rem(place, 2)
    side = lax.rem(lax.div(place, 2), 2)
    other = place + 1 - 2 * core
    sums = place < SUMS
    owner = 2 * z + 1 - side

    right, left = lax.rem(tm + 2, SEG), lax.rem(tm + 6, SEG)
    across = tm + 1 - 2 * lax.rem(tm, 2)

    beyond_side = place + 2 - 4 * side

    def in_tm(t):
        return {"tm": t, "array": place}

    def next_along_y(t):
        return {"tm": t, "array": beyond_side}

    def signal(semaphore, device):
        pl.semaphore_signal(semaphore, inc=1, device_id=device, device_id_type=MESH)

    barrier = pltpu.get_barrier_semaphore()
    for t in (left, right):
        signal(barrier, in_tm(t))
    for t in (tm, across):
        signal(barrier, next_along_y(t))
    pl.when(jnp.logical_not(sums))(lambda: signal(barrier, {"tm": tm, "array": other}))

    @pl.when(sums)
    def _():
        def greet(d, carry):
            signal(barrier, {"tm": tm, "array": lax.rem(place + 2 * d, PLACES)})
            return carry

        for k in range(0, SUMS, 2):
            signal(barrier, {"tm": tm, "array": k + 1 - core})
        lax.fori_loop(1, SIDE, greet, 0)

    inputs[0].wait()
    bands = tap_bands(taps)

    inputs[1].wait()
    filtered = decimate(raw[0], bands)

    pl.semaphore_wait(barrier, jnp.where(sums, SUMS - 1, SEG + 1) + 4)

    @pl.when(jnp.logical_not(sums))
    def _():
        for k in range(0, SUMS, 2):
            signal(column, {"tm": tm, "array": k + core})

    signal(beside, in_tm(left))
    signal(beside, next_along_y(tm))
    signal(beside, next_along_y(across))

    xall[tm] = normalize(filtered).astype(bf16)

    inputs[2].wait()
    ids = jnp.concatenate([ids_ref[r : r + 1, :] for r in range(4)], 1)
    chosen = (iota((CH, SOURCES), 0) == ids - place * CH).astype(f32).astype(bf16)
    picked = lax.dot_general(chosen, xall[tm], TN, preferred_element_type=f32)
    for t in range(SEG):
        for h in range(2):
            part = picked[ROWS * t + 8 * h : ROWS * t + 8 * h + 8]
            send0[h, t] = jnp.concatenate([part[:, :128], part[:, 128:]], 0).astype(bf16)

    halves = pltpu.make_async_remote_copy(
        send0.at[1 - core], recv0, s0_send, s0_recv, {"tm": tm, "array": other}, MESH
    )
    halves.start()

    pl.semaphore_wait(beside, 3)
    signal(beyond, in_tm(across))


    halves.wait_recv()
    for t in range(SEG):
        send1[t] = (send0[core, t].astype(f32) + recv0[t].astype(f32)).astype(bf16)

    for i in range(SEG):
        plane = jnp.where(z < 10, i // 2, 3 - i // 2)
        to_side = lax.rem(side + 1 + i, 2)
        k = plane * NYC + 2 * to_side + core
        copy = pltpu.make_async_remote_copy(
            send1.at[2 * plane + 1 - to_side], recv1.at[lax.div(lax.rem(place - k + PLACES, PLACES), 2)],
            s1_send, s1_recv, {"tm": tm, "array": k}, MESH,
        )
        pl.when(place != k)(copy.start)

    pl.semaphore_wait(beyond, 1)
    gather = [
        pltpu.make_async_remote_copy(
            xall.at[tm], xall.at[tm], x_send.at[d], x_recv.at[d], in_tm(lax.rem(tm + d, SEG)), MESH
        )
        for d in range(1, SEG)
    ]
    for copy in gather:
        copy.start()

    def announce(semaphore):
        for d in range(1, SEG):
            signal(semaphore, in_tm(lax.rem(tm + d, SEG)))

    @pl.when(sums)
    def _():
        pl.when(tm == owner)(lambda: announce(ready))
        pl.semaphore_wait(column, SIDE - SEG)
        pl.when(tm == owner)(lambda: announce(complete))

    @pl.when(sums)
    def _():
        others = recv1.at[pl.ds(1, SIDE - 1)]
        pltpu.make_async_copy(others, others, s1_recv).wait()
        total = send1[owner].astype(f32)
        for i in range(1, SIDE):
            total = total + recv1[i].astype(f32)
        mine[...] = total.astype(bf16)
        pl.when(tm != owner)(lambda: pl.semaphore_wait(ready, 1))

        def spread(p):
            copy = pltpu.make_async_remote_copy(
                mine, parts.at[core, tm], s2_send, s2_recv.at[tm], {"tm": owner, "array": p}, MESH
            )
            pl.when(jnp.logical_not((tm == owner) & (p == place)))(copy.start)

        for p in range(0, SUMS, 2):
            spread(p + 1)
            spread(p)
        pl.when(tm != owner)(lambda: pl.semaphore_wait(complete, 1))

        def one_side(i, carry):
            spread(2 * i + core)
            return carry

        lax.fori_loop(SUMS // 2, SIDE, one_side, 0)
        pl.when(tm == owner)(lambda: pltpu.make_async_copy(mine, parts.at[core, tm], s2_recv.at[tm]).start())

    step = iota((SAMPLES, CH), 0)
    for copy in gather:
        copy.wait_recv()
    for g in range(SEG):
        x = xall[g].astype(f32).T
        later = jnp.where(step == SAMPLES - 1, 0.0, pltpu.roll(x, SAMPLES - 1, 0))
        earlier = jnp.where(step == 0, 0.0, pltpu.roll(x, 1, 0))
        rhs_up[g, :, :CH] = x.astype(bf16)
        rhs_up[g, :, CH:] = later.astype(bf16)
        rhs_down[g, :, :CH] = x.astype(bf16)
        rhs_down[g, :, CH:] = earlier.astype(bf16)

    swap = pltpu.make_async_remote_copy(
        parts.at[core], parts.at[core], s3_send, s3_recv, {"tm": tm, "array": other}, MESH
    )

    @pl.when(jnp.logical_not(sums))
    def _():
        for g in range(SEG):
            pltpu.make_async_copy(mine, mine, s2_recv.at[g]).wait()
        swap.start()
        swap.wait_recv()

    lane = iota((ROWS, 128), 1)
    none = jnp.zeros((ROWS, 128), bf16)
    rising = jnp.zeros((ROWS * UP, 2 * CH), f32)
    falling = jnp.zeros((ROWS * DOWN, 2 * CH), f32)
    order = [lax.rem(g, SEG) for g in (tm, right, left, across, tm + 4, across + 2, across + 6, across + 4)]
    pair = send1.at[pl.ds(0, 2)]
    for i, g in enumerate(order):
        if i in AWAIT:

            @pl.when(sums)
            def _():
                for j in range(i, AWAIT[i]):
                    pltpu.make_async_copy(pair, pair, s2_recv.at[order[j]]).wait()

        one = parts[0, g].astype(f32)
        two = parts[1, g].astype(f32)
        low = jnp.concatenate([one[:8], two[:8]], 0).astype(bf16)
        high = jnp.concatenate([one[8:], two[8:]], 0).astype(bf16)
        later, earlier = [], []
        for i in range(UP):
            q = 2 * i
            lo, hi = (pltpu.roll(low, q, 1), pltpu.roll(high, q, 1)) if q else (low, high)
            later.append(jnp.concatenate([jnp.where(lane < q, none, lo), jnp.where(lane < q, lo, hi)], 1))
        for i in range(DOWN):
            q = 128 - (2 * i + 1)
            lo, hi = pltpu.roll(low, q, 1), pltpu.roll(high, q, 1)
            earlier.append(jnp.concatenate([jnp.where(lane < q, lo, hi), jnp.where(lane < q, hi, none)], 1))
        rising = rising + jnp.dot(jnp.concatenate(later, 0), rhs_up[g], preferred_element_type=f32)
        falling = falling + jnp.dot(jnp.concatenate(earlier, 0), rhs_down[g], preferred_element_type=f32)

    for i in range(UP):
        block = (rising[ROWS * i : ROWS * (i + 1)] * SCALE).astype(bf16)
        lag = MAXLAG + 2 * i
        out_ref[lag] = block[:, :CH]
        if lag + 1 < LAGS:
            out_ref[lag + 1] = block[:, CH:]
    for i in range(DOWN):
        block = (falling[ROWS * i : ROWS * (i + 1)] * SCALE).astype(bf16)
        lag = MAXLAG - 1 - 2 * i
        out_ref[lag] = block[:, :CH]
        out_ref[lag - 1] = block[:, CH:]

    for copy in gather + [halves]:
        copy.wait_send()

    pl.when(jnp.logical_not(sums))(swap.wait_send)

    @pl.when(jnp.logical_not(sums))
    def _():
        pltpu.make_async_copy(send1, send1, s1_send).wait()

    @pl.when(sums)
    def _():
        fewer = send1.at[pl.ds(1, SEG - 1)]
        pltpu.make_async_copy(fewer, fewer, s1_send).wait()
        others = recv1.at[pl.ds(1, USERS - 1)]
        pl.when(tm != owner)(lambda: pltpu.make_async_copy(recv1, recv1, s2_send).wait())
        pl.when(tm == owner)(lambda: pltpu.make_async_copy(others, others, s2_send).wait())


def body(raw_strain, fir_taps, source_ids):
    hbm = pl.BlockSpec(memory_space=pltpu.HBM)
    dma = pltpu.SemaphoreType.DMA
    signals = pltpu.SemaphoreType.REGULAR
    out = pl.pallas_call(
        kernel,
        out_shape=pltpu.VMEM((LAGS, ROWS, CH), bf16),
        in_specs=[hbm, hbm, hbm],
        out_specs=pl.BlockSpec(memory_space=pltpu.VMEM),
        scratch_shapes=[
            pltpu.VMEM((1, CH, RAW), bf16),
            pltpu.SMEM((NTAP,), f32),
            pltpu.VMEM((4, 32), jnp.int32),
            pltpu.VMEM((SEG, CH, SAMPLES), bf16),
            pltpu.VMEM((2, SEG, 16, 128), bf16),
            pltpu.VMEM((SEG, 16, 128), bf16),
            pltpu.VMEM((SEG, 16, 128), bf16),
            pltpu.VMEM((USERS, 16, 128), bf16),
            pltpu.VMEM((16, 128), bf16),
            pltpu.VMEM((2, SEG, 16, 128), bf16),
            pltpu.VMEM((SEG, SAMPLES, 2 * CH), bf16),
            pltpu.VMEM((SEG, SAMPLES, 2 * CH), bf16),
            dma((3,)),
            dma((SEG,)), dma((SEG,)),
            dma, dma,
            dma, dma,
            dma, dma((SEG,)),
            dma, dma,
            signals, signals, signals, signals, signals,
        ],
        compiler_params=pltpu.CompilerParams(
            collective_id=0, has_side_effects=True, vmem_limit_bytes=56 * 1024 * 1024
        ),
    )(raw_strain, fir_taps, source_ids)
    return out.transpose(1, 0, 2)


def solution(mesh):
    return jax.shard_map(
        body,
        mesh=mesh,
        in_specs=(P("tm", "array", None), P(), P()),
        out_specs=P("tm", None, "array"),
        check_vma=False,
    )
```

```python
import functools
import math

import jax
import jax.numpy as jnp
from jax import lax
from jax.experimental import pallas as pl
from jax.experimental.pallas import tpu as pltpu
from jax.sharding import PartitionSpec as P

MESH = pl.DeviceIdType.MESH
SOURCES = 128
MAXLAG = 50
WINDOW = 64
DECIM = 4
NTAP = 8
SAMPLES = 256
LAGS = 101
RAW = 1024
SEG = 8
ROWS = 16
CH = 128
NZ = 16
NYC = 4
PLACES = NZ * NYC
SUMS = 16
SIDE = PLACES // 2
ORDER = (0, 1, 4, 5, 2, 3, 6, 10, 7, 9, 8, 11, 12, 13, 14, 15)
AWAIT = {0: 4, 4: 8}
USERS = SUMS + (PLACES - SUMS) // 2
UP = 26
DOWN = 25
EPSILON = 1e-05
SCALE = 1.0 / (math.sqrt(SAMPLES) * math.sqrt(SEG))

f32 = jnp.float32
bf16 = jnp.bfloat16
TN = (((0,), (0,)), ((), ()))


def iota(shape, dim):
    return lax.broadcasted_iota(jnp.int32, shape, dim)


def terms(value, count):
    parts = []
    for _ in range(count):
        part = value.astype(bf16)
        parts.append(part)
        value = value - part.astype(f32)
    return parts


def tap_bands(taps_ref):
    k = DECIM * iota((128, 128), 1) - iota((128, 128), 0)
    band = jnp.zeros((128, 128), f32)
    for tap in range(NTAP):
        band = jnp.where(k == tap, taps_ref[tap], band)
    band = jnp.concatenate([band, jnp.zeros((128, 128), f32)], 1)
    lane = iota((128, SAMPLES), 1)
    bands = []
    for tile in range(RAW // 128):
        placed = pltpu.roll(band, 32 * tile, 1) if tile else band
        if tile == RAW // 128 - 1:
            placed = jnp.where(lane < 2, 0.0, placed)
        bands.append(terms(placed, 3))
    return bands


def decimate(raw, bands):
    filtered = jnp.zeros((CH, SAMPLES), f32)
    for term in range(3):
        matrix = jnp.concatenate([band[term] for band in bands], 0)
        filtered = filtered + jnp.dot(raw, matrix, preferred_element_type=f32)
    return filtered


def window_matrix():
    gap = iota((SAMPLES, SAMPLES), 0) - iota((SAMPLES, SAMPLES), 1)
    return jnp.where((gap >= -(WINDOW // 2)) & (gap < WINDOW // 2), 1.0, 0.0).astype(bf16)


def normalize(filtered, window):
    total = jnp.zeros((CH, SAMPLES), f32)
    for part in terms(jnp.abs(filtered), 2):
        total = total + jnp.dot(part, window, preferred_element_type=f32)
    return filtered / (total * (1.0 / WINDOW) + EPSILON)


def kernel(
    raw_hbm, taps_hbm, ids_hbm, out_ref,
    raw, taps, ids_ref, xall, send0, recv0, send1, recv1, mine, parts, rhs_up, rhs_down,
    in_sem, x_send, x_recv, s0_send, s0_recv, s1_send, s1_recv, s2_send, s2_recv, s3_send, s3_recv, column, beside, beyond, ready, complete,
):
    inputs = [
        pltpu.make_async_copy(src, dst, in_sem.at[i])
        for i, (src, dst) in enumerate(((raw_hbm, raw), (taps_hbm, taps), (ids_hbm, ids_ref)))
    ]
    for copy in inputs:
        copy.start()

    tm = lax.axis_index("tm")
    place = lax.axis_index("array")
    z = lax.div(place, NYC)
    core = lax.rem(place, 2)
    side = lax.rem(lax.div(place, 2), 2)
    other = place + 1 - 2 * core
    sums = place < SUMS
    owner = 2 * z + 1 - side

    right, left = lax.rem(tm + 2, SEG), lax.rem(tm + 6, SEG)
    across = tm + 1 - 2 * lax.rem(tm, 2)

    beyond_side = place + 2 - 4 * side

    def in_tm(t):
        return {"tm": t, "array": place}

    def next_along_y(t):
        return {"tm": t, "array": beyond_side}

    def signal(semaphore, device):
        pl.semaphore_signal(semaphore, inc=1, device_id=device, device_id_type=MESH)

    barrier = pltpu.get_barrier_semaphore()
    for t in (left, right):
        signal(barrier, in_tm(t))
    for t in (tm, across):
        signal(barrier, next_along_y(t))
    pl.when(jnp.logical_not(sums))(lambda: signal(barrier, {"tm": tm, "array": other}))

    @pl.when(sums)
    def _():
        def greet(d, carry):
            signal(barrier, {"tm": tm, "array": lax.rem(place + 2 * d, PLACES)})
            return carry

        for k in range(0, SUMS, 2):
            signal(barrier, {"tm": tm, "array": k + 1 - core})
        lax.fori_loop(1, SIDE, greet, 0)

    inputs[1].wait()
    bands = tap_bands(taps)

    window = window_matrix()

    inputs[2].wait()
    ids = jnp.concatenate([ids_ref[r : r + 1, :] for r in range(4)], 1)
    chosen = (iota((CH, SOURCES), 0) == ids - place * CH).astype(f32).astype(bf16)

    inputs[0].wait()
    filtered = decimate(raw[0], bands)

    pl.semaphore_wait(barrier, jnp.where(sums, SUMS - 1, SEG + 1) + 4)

    mine_at = lax.div(tm, 2) * NYC + 2 * (1 - lax.rem(tm, 2)) + core
    pl.when(jnp.logical_not(sums))(lambda: signal(column, {"tm": tm, "array": mine_at}))

    xall[tm] = normalize(filtered, window).astype(bf16)

    picked = lax.dot_general(chosen, xall[tm], TN, preferred_element_type=f32)
    for t in range(SEG):
        for h in range(2):
            part = picked[ROWS * t + 8 * h : ROWS * t + 8 * h + 8]
            send0[h, t] = jnp.concatenate([part[:, :128], part[:, 128:]], 0).astype(bf16)

    halves = pltpu.make_async_remote_copy(
        send0.at[1 - core], recv0, s0_send, s0_recv, {"tm": tm, "array": other}, MESH
    )
    halves.start()

    signal(beside, in_tm(left))
    signal(beside, next_along_y(tm))
    signal(beside, next_along_y(across))

    halves.wait_recv()
    for t in range(SEG):
        send1[t] = (send0[core, t].astype(f32) + recv0[t].astype(f32)).astype(bf16)

    for i in range(SEG):
        plane = jnp.where(z < 10, i // 2, 3 - i // 2)
        to_side = lax.rem(side + 1 + i, 2)
        k = plane * NYC + 2 * to_side + core
        copy = pltpu.make_async_remote_copy(
            send1.at[2 * plane + 1 - to_side], recv1.at[lax.div(lax.rem(place - k + PLACES, PLACES), 2)],
            s1_send, s1_recv, {"tm": tm, "array": k}, MESH,
        )
        pl.when(place != k)(copy.start)

    pl.semaphore_wait(beside, 3)
    signal(beyond, in_tm(across))
    pl.semaphore_wait(beyond, 1)
    gather = [
        pltpu.make_async_remote_copy(
            xall.at[tm], xall.at[tm], x_send.at[d], x_recv.at[d], in_tm(lax.rem(tm + d, SEG)), MESH
        )
        for d in range(1, SEG)
    ]
    for copy in gather:
        copy.start()

    def announce(semaphore):
        for d in range(1, SEG):
            signal(semaphore, in_tm(lax.rem(tm + d, SEG)))

    @pl.when(sums & (tm == owner))
    def _():
        announce(ready)
        pl.semaphore_wait(column, SIDE - SEG)
        announce(complete)

    @pl.when(sums)
    def _():
        others = recv1.at[pl.ds(1, SIDE - 1)]
        pltpu.make_async_copy(others, others, s1_recv).wait()
        total = send1[owner].astype(f32)
        for i in range(1, SIDE):
            total = total + recv1[i].astype(f32)
        mine[...] = total.astype(bf16)
        pl.when(tm != owner)(lambda: pl.semaphore_wait(ready, 1))

        def spread(p):
            return pltpu.make_async_remote_copy(
                mine, parts.at[core, tm], s2_send, s2_recv.at[tm], {"tm": owner, "array": p}, MESH
            )

        for z_to in ORDER:
            if z_to == ORDER[2]:
                pl.when(tm != owner)(lambda: pl.semaphore_wait(complete, 1))
            for side_to in range(2):
                p = z_to * NYC + 2 * side_to
                if p < SUMS:
                    for q in (p + 1, p):
                        pl.when(jnp.logical_not((tm == owner) & (place == q)))(spread(q).start)
                else:
                    spread(p + core).start()
        pl.when(tm == owner)(lambda: pltpu.make_async_copy(mine, parts.at[core, tm], s2_recv.at[tm]).start())

    step = iota((SAMPLES, CH), 0)
    for copy in gather:
        copy.wait_recv()
    for g in range(SEG):
        x = xall[g].astype(f32).T
        later = jnp.where(step == SAMPLES - 1, 0.0, pltpu.roll(x, SAMPLES - 1, 0))
        earlier = jnp.where(step == 0, 0.0, pltpu.roll(x, 1, 0))
        rhs_up[g, :, :CH] = x.astype(bf16)
        rhs_up[g, :, CH:] = later.astype(bf16)
        rhs_down[g, :, :CH] = x.astype(bf16)
        rhs_down[g, :, CH:] = earlier.astype(bf16)

    swap = pltpu.make_async_remote_copy(
        parts.at[core], parts.at[core], s3_send, s3_recv, {"tm": tm, "array": other}, MESH
    )

    @pl.when(jnp.logical_not(sums))
    def _():
        for g in range(SEG):
            pltpu.make_async_copy(mine, mine, s2_recv.at[g]).wait()
        swap.start()
        swap.wait_recv()

    lane = iota((ROWS, 128), 1)
    none = jnp.zeros((ROWS, 128), bf16)
    rising = jnp.zeros((ROWS * UP, 2 * CH), f32)
    falling = jnp.zeros((ROWS * DOWN, 2 * CH), f32)
    order = [lax.rem(g, SEG) for g in (tm, right, left, across, tm + 4, across + 2, across + 6, across + 4)]
    pair = send1.at[pl.ds(0, 2)]
    for i, g in enumerate(order):
        if i in AWAIT:

            @pl.when(sums)
            def _():
                for j in range(i, AWAIT[i]):
                    pltpu.make_async_copy(pair, pair, s2_recv.at[order[j]]).wait()

        one = parts[0, g].astype(f32)
        two = parts[1, g].astype(f32)
        low = jnp.concatenate([one[:8], two[:8]], 0).astype(bf16)
        high = jnp.concatenate([one[8:], two[8:]], 0).astype(bf16)
        later, earlier = [], []
        for i in range(UP):
            q = 2 * i
            lo, hi = (pltpu.roll(low, q, 1), pltpu.roll(high, q, 1)) if q else (low, high)
            later.append(jnp.concatenate([jnp.where(lane < q, none, lo), jnp.where(lane < q, lo, hi)], 1))
        for i in range(DOWN):
            q = 128 - (2 * i + 1)
            lo, hi = pltpu.roll(low, q, 1), pltpu.roll(high, q, 1)
            earlier.append(jnp.concatenate([jnp.where(lane < q, lo, hi), jnp.where(lane < q, hi, none)], 1))
        rising = rising + jnp.dot(jnp.concatenate(later, 0), rhs_up[g], preferred_element_type=f32)
        falling = falling + jnp.dot(jnp.concatenate(earlier, 0), rhs_down[g], preferred_element_type=f32)

    for i in range(UP):
        block = (rising[ROWS * i : ROWS * (i + 1)] * SCALE).astype(bf16)
        lag = MAXLAG + 2 * i
        out_ref[lag] = block[:, :CH]
        if lag + 1 < LAGS:
            out_ref[lag + 1] = block[:, CH:]
    for i in range(DOWN):
        block = (falling[ROWS * i : ROWS * (i + 1)] * SCALE).astype(bf16)
        lag = MAXLAG - 1 - 2 * i
        out_ref[lag] = block[:, :CH]
        out_ref[lag - 1] = block[:, CH:]

    for copy in gather + [halves]:
        copy.wait_send()

    pl.when(jnp.logical_not(sums))(swap.wait_send)

    @pl.when(jnp.logical_not(sums))
    def _():
        pltpu.make_async_copy(send1, send1, s1_send).wait()

    @pl.when(sums)
    def _():
        fewer = send1.at[pl.ds(1, SEG - 1)]
        pltpu.make_async_copy(fewer, fewer, s1_send).wait()
        others = recv1.at[pl.ds(1, USERS - 1)]
        pl.when(tm != owner)(lambda: pltpu.make_async_copy(recv1, recv1, s2_send).wait())
        pl.when(tm == owner)(lambda: pltpu.make_async_copy(others, others, s2_send).wait())


def body(raw_strain, fir_taps, source_ids):
    hbm = pl.BlockSpec(memory_space=pltpu.HBM)
    dma = pltpu.SemaphoreType.DMA
    signals = pltpu.SemaphoreType.REGULAR
    out = pl.pallas_call(
        kernel,
        out_shape=pltpu.VMEM((LAGS, ROWS, CH), bf16),
        in_specs=[hbm, hbm, hbm],
        out_specs=pl.BlockSpec(memory_space=pltpu.VMEM),
        scratch_shapes=[
            pltpu.VMEM((1, CH, RAW), bf16),
            pltpu.SMEM((NTAP,), f32),
            pltpu.VMEM((4, 32), jnp.int32),
            pltpu.VMEM((SEG, CH, SAMPLES), bf16),
            pltpu.VMEM((2, SEG, 16, 128), bf16),
            pltpu.VMEM((SEG, 16, 128), bf16),
            pltpu.VMEM((SEG, 16, 128), bf16),
            pltpu.VMEM((USERS, 16, 128), bf16),
            pltpu.VMEM((16, 128), bf16),
            pltpu.VMEM((2, SEG, 16, 128), bf16),
            pltpu.VMEM((SEG, SAMPLES, 2 * CH), bf16),
            pltpu.VMEM((SEG, SAMPLES, 2 * CH), bf16),
            dma((3,)),
            dma((SEG,)), dma((SEG,)),
            dma, dma,
            dma, dma,
            dma, dma((SEG,)),
            dma, dma,
            signals, signals, signals, signals, signals,
        ],
        compiler_params=pltpu.CompilerParams(
            collective_id=0, has_side_effects=True, vmem_limit_bytes=56 * 1024 * 1024
        ),
    )(raw_strain, fir_taps, source_ids)
    return out.transpose(1, 0, 2)


def solution(mesh):
    return jax.shard_map(
        body,
        mesh=mesh,
        in_specs=(P("tm", "array", None), P(), P()),
        out_specs=P("tm", None, "array"),
        check_vma=False,
    )
```

```python
import functools
import math

import jax
import jax.numpy as jnp
from jax import lax
from jax.experimental import pallas as pl
from jax.experimental.pallas import tpu as pltpu
from jax.sharding import PartitionSpec as P

MESH = pl.DeviceIdType.MESH
SOURCES = 128
MAXLAG = 50
WINDOW = 64
DECIM = 4
NTAP = 8
SAMPLES = 256
LAGS = 101
RAW = 1024
SEG = 8
ROWS = 16
CH = 128
NZ = 16
NYC = 4
PLACES = NZ * NYC
FIRST = 1
SUMS = 16
SIDE = PLACES // 2
ORDER = (0, 1, 4, 5, 2, 6, 9, 10, 3, 7, 8, 11, 12, 13, 14, 15)
USERS = SUMS + (PLACES - SUMS) // 2
UP = 26
DOWN = 25
EPSILON = 1e-05
SCALE = 1.0 / (math.sqrt(SAMPLES) * math.sqrt(SEG))

f32 = jnp.float32
bf16 = jnp.bfloat16
TN = (((0,), (0,)), ((), ()))


def iota(shape, dim):
    return lax.broadcasted_iota(jnp.int32, shape, dim)


def terms(value, count):
    parts = []
    for _ in range(count):
        part = value.astype(bf16)
        parts.append(part)
        value = value - part.astype(f32)
    return parts


def tap_bands(taps_ref):
    k = DECIM * iota((128, 128), 1) - iota((128, 128), 0)
    band = jnp.zeros((128, 128), f32)
    for tap in range(NTAP):
        band = jnp.where(k == tap, taps_ref[tap], band)
    band = jnp.concatenate([band, jnp.zeros((128, 128), f32)], 1)
    lane = iota((128, SAMPLES), 1)
    bands = []
    for tile in range(RAW // 128):
        placed = pltpu.roll(band, 32 * tile, 1) if tile else band
        if tile == RAW // 128 - 1:
            placed = jnp.where(lane < 2, 0.0, placed)
        bands.append(terms(placed, 3))
    return bands


def decimate(raw, bands):
    filtered = jnp.zeros((CH, SAMPLES), f32)
    for term in range(3):
        matrix = jnp.concatenate([band[term] for band in bands], 0)
        filtered = filtered + jnp.dot(raw, matrix, preferred_element_type=f32)
    return filtered


def window_matrix():
    gap = iota((SAMPLES, SAMPLES), 0) - iota((SAMPLES, SAMPLES), 1)
    return jnp.where((gap >= -(WINDOW // 2)) & (gap < WINDOW // 2), 1.0, 0.0).astype(bf16)


def normalize(filtered, window):
    total = jnp.zeros((CH, SAMPLES), f32)
    for part in terms(jnp.abs(filtered), 2):
        total = total + jnp.dot(part, window, preferred_element_type=f32)
    return filtered / (total * (1.0 / WINDOW) + EPSILON)


def kernel(
    raw_hbm, taps_hbm, ids_hbm, out_ref,
    raw, taps, ids_ref, xall, send0, recv0, send1, recv1, mine, parts, rhs_up, rhs_down,
    in_sem, x_send, x_recv, s0_send, s0_recv, s1_send, s1_recv, s2_send, s2_recv, s3_send, s3_recv, column, beside, beyond, ready, complete,
):
    inputs = [
        pltpu.make_async_copy(src, dst, in_sem.at[i])
        for i, (src, dst) in enumerate(((raw_hbm, raw), (taps_hbm, taps), (ids_hbm, ids_ref)))
    ]
    for copy in inputs:
        copy.start()

    tm = lax.axis_index("tm")
    place = lax.axis_index("array")
    z = lax.div(place, NYC)
    core = lax.rem(place, 2)
    side = lax.rem(lax.div(place, 2), 2)
    other = place + 1 - 2 * core
    sums = place < SUMS
    owner = 2 * z + 1 - side
    both = sums & (side == 1) & (z < FIRST)

    right, left = lax.rem(tm + 2, SEG), lax.rem(tm + 6, SEG)
    across = tm + 1 - 2 * lax.rem(tm, 2)

    beyond_side = place + 2 - 4 * side

    def in_tm(t):
        return {"tm": t, "array": place}

    def next_along_y(t):
        return {"tm": t, "array": beyond_side}

    def signal(semaphore, device):
        pl.semaphore_signal(semaphore, inc=1, device_id=device, device_id_type=MESH)

    barrier = pltpu.get_barrier_semaphore()
    for t in (left, right):
        signal(barrier, in_tm(t))
    for t in (tm, across):
        signal(barrier, next_along_y(t))
    pl.when(jnp.logical_not(sums))(lambda: signal(barrier, {"tm": tm, "array": other}))

    @pl.when(sums)
    def _():
        def greet(d, carry):
            signal(barrier, {"tm": tm, "array": lax.rem(place + 2 * d, PLACES)})
            return carry

        def greet_other(d, carry):
            signal(barrier, {"tm": tm, "array": lax.rem(other + 2 * d, PLACES)})
            return carry

        @pl.when(jnp.logical_not(both))
        def _():
            for k in range(0, SUMS, 2):
                signal(barrier, {"tm": tm, "array": k + 1 - core})

        @pl.when(both)
        def _():
            lax.fori_loop(0, SIDE, greet_other, 0)

        lax.fori_loop(1, SIDE, greet, 0)

    inputs[1].wait()
    bands = tap_bands(taps)

    window = window_matrix()

    inputs[2].wait()
    ids = jnp.concatenate([ids_ref[r : r + 1, :] for r in range(4)], 1)
    chosen = (iota((CH, SOURCES), 0) == ids - place * CH).astype(f32).astype(bf16)

    inputs[0].wait()
    filtered = decimate(raw[0], bands)

    pl.semaphore_wait(barrier, jnp.where(sums, SUMS - 1, SEG + FIRST + 1) + 4)

    mine_at = lax.div(tm, 2) * NYC + 2 * (1 - lax.rem(tm, 2)) + core
    pl.when(jnp.logical_not(sums))(lambda: signal(column, {"tm": tm, "array": mine_at}))

    xall[tm] = normalize(filtered, window).astype(bf16)

    picked = lax.dot_general(chosen, xall[tm], TN, preferred_element_type=f32)
    for t in range(SEG):
        for h in range(2):
            part = picked[ROWS * t + 8 * h : ROWS * t + 8 * h + 8]
            send0[h, t // 2 + 4 * (t % 2)] = jnp.concatenate([part[:, :128], part[:, 128:]], 0).astype(bf16)

    halves = pltpu.make_async_remote_copy(
        send0.at[1 - core, pl.ds(FIRST, SEG - FIRST)], recv0, s0_send, s0_recv, {"tm": tm, "array": other}, MESH
    )
    halves.start()

    def to_sum(chunk, k):
        slot = lax.rem(place - k + PLACES, PLACES)
        return pltpu.make_async_remote_copy(
            chunk, recv1.at[slot], s1_send, s1_recv, {"tm": tm, "array": k}, MESH
        )

    for plane in range(FIRST):
        k = plane * NYC + 2 + core
        pl.when(place != k)(to_sum(send0.at[core, plane], k).start)
        to_sum(send0.at[1 - core, plane], plane * NYC + 3 - core).start()

    signal(beside, in_tm(left))
    signal(beside, next_along_y(tm))
    signal(beside, next_along_y(across))

    halves.wait_recv()
    rest = [4, 1, 5, 2, 6, 3, 7]
    for near, far in zip(rest, reversed(rest), strict=True):
        chunk = jnp.where(z < 10, near, far)
        i = chunk - FIRST
        k = jnp.where(chunk < 4, chunk * NYC + 2, (chunk - 4) * NYC) + core
        send1[i] = (send0[core, chunk].astype(f32) + recv0[i].astype(f32)).astype(bf16)
        pl.when(place != k)(to_sum(send1.at[i], k).start)

    pl.semaphore_wait(beside, 3)
    signal(beyond, in_tm(across))
    pl.semaphore_wait(beyond, 1)
    gather = [
        pltpu.make_async_remote_copy(
            xall.at[tm], xall.at[tm], x_send.at[d], x_recv.at[d], in_tm(lax.rem(tm + d, SEG)), MESH
        )
        for d in range(1, SEG)
    ]
    for copy in gather:
        copy.start()

    def announce(semaphore):
        for d in range(1, SEG):
            signal(semaphore, in_tm(lax.rem(tm + d, SEG)))

    @pl.when(sums & (tm == owner))
    def _():
        announce(ready)
        pl.semaphore_wait(column, SIDE - SEG)
        announce(complete)

    @pl.when(sums)
    def _():

        @pl.when(jnp.logical_not(both))
        def _():
            others = recv1.at[pl.ds(0, SIDE - 1)]
            pltpu.make_async_copy(others, others, s1_recv).wait()
            total = send1[jnp.where(side == 1, z, z + 4) - FIRST].astype(f32)
            for i in range(2, PLACES, 2):
                total = total + recv1[i].astype(f32)
            mine[...] = total.astype(bf16)

        @pl.when(both)
        def _():
            others = recv1.at[pl.ds(0, PLACES - 1)]
            pltpu.make_async_copy(others, others, s1_recv).wait()
            total = send0[core, z].astype(f32)
            for i in range(1, PLACES):
                total = total + recv1[i].astype(f32)
            mine[...] = total.astype(bf16)

        pl.when(tm != owner)(lambda: pl.semaphore_wait(ready, 1))

        def spread(p):
            return pltpu.make_async_remote_copy(
                mine, parts.at[core, tm], s2_send, s2_recv.at[tm], {"tm": owner, "array": p}, MESH
            )

        for z_to in ORDER:
            if z_to == ORDER[2]:
                pl.when(tm != owner)(lambda: pl.semaphore_wait(complete, 1))
            for side_to in range(2):
                p = z_to * NYC + 2 * side_to
                if p < SUMS:
                    for q in (p + 1, p):
                        pl.when(jnp.logical_not((tm == owner) & (place == q)))(spread(q).start)
                else:
                    spread(p + core).start()
        pl.when(tm == owner)(lambda: pltpu.make_async_copy(mine, parts.at[core, tm], s2_recv.at[tm]).start())

    step = iota((SAMPLES, CH), 0)
    for copy in gather:
        copy.wait_recv()
    for g in range(SEG):
        x = xall[g].astype(f32).T
        later = jnp.where(step == SAMPLES - 1, 0.0, pltpu.roll(x, SAMPLES - 1, 0))
        earlier = jnp.where(step == 0, 0.0, pltpu.roll(x, 1, 0))
        rhs_up[g, :, :CH] = x.astype(bf16)
        rhs_up[g, :, CH:] = later.astype(bf16)
        rhs_down[g, :, :CH] = x.astype(bf16)
        rhs_down[g, :, CH:] = earlier.astype(bf16)

    swap = pltpu.make_async_remote_copy(
        parts.at[core], parts.at[core], s3_send, s3_recv, {"tm": tm, "array": other}, MESH
    )

    @pl.when(jnp.logical_not(sums))
    def _():
        for g in range(SEG):
            pltpu.make_async_copy(mine, mine, s2_recv.at[g]).wait()
        swap.start()
        swap.wait_recv()

    lane = iota((ROWS, 128), 1)
    none = jnp.zeros((ROWS, 128), bf16)

    def later(low, high):
        rows = []
        for i in range(UP):
            q = 2 * i
            lo, hi = (pltpu.roll(low, q, 1), pltpu.roll(high, q, 1)) if q else (low, high)
            rows.append(jnp.concatenate([jnp.where(lane < q, none, lo), jnp.where(lane < q, lo, hi)], 1))
        return jnp.concatenate(rows, 0)

    def earlier(low, high):
        rows = []
        for i in range(DOWN):
            q = 128 - (2 * i + 1)
            lo, hi = pltpu.roll(low, q, 1), pltpu.roll(high, q, 1)
            rows.append(jnp.concatenate([jnp.where(lane < q, lo, hi), jnp.where(lane < q, hi, none)], 1))
        return jnp.concatenate(rows, 0)

    order = [lax.rem(g, SEG) for g in (tm, right, left, across, tm + 4, across + 2, across + 6, across + 4)]
    pair = send1.at[pl.ds(0, 2)]
    rising = jnp.zeros((ROWS * UP, 2 * CH), f32)
    falling = jnp.zeros((ROWS * DOWN, 2 * CH), f32)
    for group in (order[: SEG // 2], order[SEG // 2 :]):

        @pl.when(sums)
        def _():
            for g in group:
                pltpu.make_async_copy(pair, pair, s2_recv.at[g]).wait()

        halves_of = []
        for g in group:
            one = parts[0, g].astype(f32)
            two = parts[1, g].astype(f32)
            low = jnp.concatenate([one[:8], two[:8]], 0).astype(bf16)
            high = jnp.concatenate([one[8:], two[8:]], 0).astype(bf16)
            halves_of.append((low, high))
        for g, lh in zip(group, halves_of, strict=True):
            rising = rising + jnp.dot(later(*lh), rhs_up[g], preferred_element_type=f32)
        for g, lh in zip(group, halves_of, strict=True):
            falling = falling + jnp.dot(earlier(*lh), rhs_down[g], preferred_element_type=f32)

    for i in range(UP):
        block = (rising[ROWS * i : ROWS * (i + 1)] * SCALE).astype(bf16)
        lag = MAXLAG + 2 * i
        out_ref[lag] = block[:, :CH]
        if lag + 1 < LAGS:
            out_ref[lag + 1] = block[:, CH:]
    for i in range(DOWN):
        block = (falling[ROWS * i : ROWS * (i + 1)] * SCALE).astype(bf16)
        lag = MAXLAG - 1 - 2 * i
        out_ref[lag] = block[:, :CH]
        out_ref[lag - 1] = block[:, CH:]

    for copy in gather + [halves]:
        copy.wait_send()

    pl.when(jnp.logical_not(sums))(swap.wait_send)

    @pl.when(jnp.logical_not(sums))
    def _():
        sent = recv1.at[pl.ds(0, SEG + FIRST)]
        pltpu.make_async_copy(sent, sent, s1_send).wait()

    @pl.when(sums)
    def _():
        sent = recv1.at[pl.ds(0, SEG + FIRST - 1)]
        pltpu.make_async_copy(sent, sent, s1_send).wait()
        users = recv1.at[pl.ds(0, USERS)]
        others = recv1.at[pl.ds(0, USERS - 1)]
        pl.when(tm != owner)(lambda: pltpu.make_async_copy(users, users, s2_send).wait())
        pl.when(tm == owner)(lambda: pltpu.make_async_copy(others, others, s2_send).wait())


def body(raw_strain, fir_taps, source_ids):
    hbm = pl.BlockSpec(memory_space=pltpu.HBM)
    dma = pltpu.SemaphoreType.DMA
    signals = pltpu.SemaphoreType.REGULAR
    out = pl.pallas_call(
        kernel,
        out_shape=pltpu.VMEM((LAGS, ROWS, CH), bf16),
        in_specs=[hbm, hbm, hbm],
        out_specs=pl.BlockSpec(memory_space=pltpu.VMEM),
        scratch_shapes=[
            pltpu.VMEM((1, CH, RAW), bf16),
            pltpu.SMEM((NTAP,), f32),
            pltpu.VMEM((4, 32), jnp.int32),
            pltpu.VMEM((SEG, CH, SAMPLES), bf16),
            pltpu.VMEM((2, SEG, 16, 128), bf16),
            pltpu.VMEM((SEG - FIRST, 16, 128), bf16),
            pltpu.VMEM((SEG - FIRST, 16, 128), bf16),
            pltpu.VMEM((PLACES, 16, 128), bf16),
            pltpu.VMEM((16, 128), bf16),
            pltpu.VMEM((2, SEG, 16, 128), bf16),
            pltpu.VMEM((SEG, SAMPLES, 2 * CH), bf16),
            pltpu.VMEM((SEG, SAMPLES, 2 * CH), bf16),
            dma((3,)),
            dma((SEG,)), dma((SEG,)),
            dma, dma,
            dma, dma,
            dma, dma((SEG,)),
            dma, dma,
            signals, signals, signals, signals, signals,
        ],
        compiler_params=pltpu.CompilerParams(
            collective_id=0, has_side_effects=True, vmem_limit_bytes=56 * 1024 * 1024
        ),
    )(raw_strain, fir_taps, source_ids)
    return out.transpose(1, 0, 2)


def solution(mesh):
    return jax.shard_map(
        body,
        mesh=mesh,
        in_specs=(P("tm", "array", None), P(), P()),
        out_specs=P("tm", None, "array"),
        check_vma=False,
    )
```

```python
import functools
import math

import jax
import jax.numpy as jnp
from jax import lax
from jax.experimental import pallas as pl
from jax.experimental.pallas import tpu as pltpu
from jax.sharding import PartitionSpec as P

MESH = pl.DeviceIdType.MESH
SOURCES = 128
MAXLAG = 50
WINDOW = 64
DECIM = 4
NTAP = 8
SAMPLES = 256
LAGS = 101
RAW = 1024
SEG = 8
ROWS = 16
CH = 128
NZ = 16
NYC = 4
PLACES = NZ * NYC
FIRST = 1
SUMS = 16
SIDE = PLACES // 2
ORDER = (0, 1, 4, 5, 2, 6, 9, 10, 3, 7, 8, 11, 12, 13, 14, 15)
USERS = SUMS + (PLACES - SUMS) // 2
UP = 26
DOWN = 25
EPSILON = 1e-05
SCALE = 1.0 / (math.sqrt(SAMPLES) * math.sqrt(SEG))

f32 = jnp.float32
bf16 = jnp.bfloat16
TN = (((0,), (0,)), ((), ()))


def iota(shape, dim):
    return lax.broadcasted_iota(jnp.int32, shape, dim)


def terms(value, count):
    parts = []
    for _ in range(count):
        part = value.astype(bf16)
        parts.append(part)
        value = value - part.astype(f32)
    return parts


def tap_bands(taps_ref):
    k = DECIM * iota((128, 128), 1) - iota((128, 128), 0)
    band = jnp.zeros((128, 128), f32)
    for tap in range(NTAP):
        band = jnp.where(k == tap, taps_ref[tap], band)
    band = jnp.concatenate([band, jnp.zeros((128, 128), f32)], 1)
    lane = iota((128, SAMPLES), 1)
    bands = []
    for tile in range(RAW // 128):
        placed = pltpu.roll(band, 32 * tile, 1) if tile else band
        if tile == RAW // 128 - 1:
            placed = jnp.where(lane < 2, 0.0, placed)
        bands.append(terms(placed, 3))
    return bands


def decimate(raw, bands):
    filtered = jnp.zeros((CH, SAMPLES), f32)
    for term in range(3):
        matrix = jnp.concatenate([band[term] for band in bands], 0)
        filtered = filtered + jnp.dot(raw, matrix, preferred_element_type=f32)
    return filtered


def window_matrix():
    gap = iota((SAMPLES, SAMPLES), 0) - iota((SAMPLES, SAMPLES), 1)
    return jnp.where((gap >= -(WINDOW // 2)) & (gap < WINDOW // 2), 1.0, 0.0).astype(bf16)


def normalize(filtered, window):
    total = jnp.zeros((CH, SAMPLES), f32)
    for part in terms(jnp.abs(filtered), 2):
        total = total + jnp.dot(part, window, preferred_element_type=f32)
    return filtered / (total * (1.0 / WINDOW) + EPSILON)


def kernel(
    raw_hbm, taps_hbm, ids_hbm, out_ref,
    raw, taps, ids_ref, xall, send0, recv0, send1, recv1, mine, parts, rhs_up, rhs_down,
    in_sem, x_send, x_recv, s0_send, s0_recv, s1_send, s1_recv, s2_send, s2_recv, s3_send, s3_recv, column, beside, beyond, ready, complete,
):
    inputs = [
        pltpu.make_async_copy(src, dst, in_sem.at[i])
        for i, (src, dst) in enumerate(((raw_hbm, raw), (taps_hbm, taps), (ids_hbm, ids_ref)))
    ]
    for copy in inputs:
        copy.start()

    tm = lax.axis_index("tm")
    place = lax.axis_index("array")
    z = lax.div(place, NYC)
    core = lax.rem(place, 2)
    side = lax.rem(lax.div(place, 2), 2)
    other = place + 1 - 2 * core
    sums = place < SUMS
    owner = 2 * z + 1 - side
    both = sums & (side == 1) & (z < FIRST)

    right, left = lax.rem(tm + 2, SEG), lax.rem(tm + 6, SEG)
    across = tm + 1 - 2 * lax.rem(tm, 2)

    beyond_side = place + 2 - 4 * side

    def in_tm(t):
        return {"tm": t, "array": place}

    def next_along_y(t):
        return {"tm": t, "array": beyond_side}

    def signal(semaphore, device):
        pl.semaphore_signal(semaphore, inc=1, device_id=device, device_id_type=MESH)

    barrier = pltpu.get_barrier_semaphore()
    for t in (left, right):
        signal(barrier, in_tm(t))
    for t in (tm, across):
        signal(barrier, next_along_y(t))
    pl.when(jnp.logical_not(sums))(lambda: signal(barrier, {"tm": tm, "array": other}))

    @pl.when(sums)
    def _():
        def greet(d, carry):
            signal(barrier, {"tm": tm, "array": lax.rem(place + 2 * d, PLACES)})
            return carry

        def greet_other(d, carry):
            signal(barrier, {"tm": tm, "array": lax.rem(other + 2 * d, PLACES)})
            return carry

        @pl.when(jnp.logical_not(both))
        def _():
            for k in range(0, SUMS, 2):
                signal(barrier, {"tm": tm, "array": k + 1 - core})

        @pl.when(both)
        def _():
            lax.fori_loop(0, SIDE, greet_other, 0)

        lax.fori_loop(1, SIDE, greet, 0)

    inputs[1].wait()
    bands = tap_bands(taps)

    window = window_matrix()

    inputs[2].wait()
    ids = jnp.concatenate([ids_ref[r : r + 1, :] for r in range(4)], 1)
    chosen = (iota((CH, SOURCES), 0) == ids - place * CH).astype(f32).astype(bf16)

    inputs[0].wait()
    filtered = decimate(raw[0], bands)

    pl.semaphore_wait(barrier, jnp.where(sums, SUMS - 1, SEG + FIRST + 1) + 4)

    mine_at = lax.div(tm, 2) * NYC + 2 * (1 - lax.rem(tm, 2)) + core
    pl.when(jnp.logical_not(sums))(lambda: signal(column, {"tm": tm, "array": mine_at}))

    xall[tm] = normalize(filtered, window).astype(bf16)

    picked = lax.dot_general(chosen, xall[tm], TN, preferred_element_type=f32)
    for t in range(SEG):
        for h in range(2):
            part = picked[ROWS * t + 8 * h : ROWS * t + 8 * h + 8]
            send0[h, t // 2 + 4 * (t % 2)] = jnp.concatenate([part[:, :128], part[:, 128:]], 0).astype(bf16)

    halves = pltpu.make_async_remote_copy(
        send0.at[1 - core, pl.ds(FIRST, SEG - FIRST)], recv0, s0_send, s0_recv, {"tm": tm, "array": other}, MESH
    )
    halves.start()

    def to_sum(chunk, k):
        slot = lax.rem(place - k + PLACES, PLACES)
        return pltpu.make_async_remote_copy(
            chunk, recv1.at[slot], s1_send, s1_recv, {"tm": tm, "array": k}, MESH
        )

    for plane in range(FIRST):
        k = plane * NYC + 2 + core
        pl.when(place != k)(to_sum(send0.at[core, plane], k).start)
        to_sum(send0.at[1 - core, plane], plane * NYC + 3 - core).start()

    signal(beside, in_tm(left))
    signal(beside, next_along_y(tm))
    signal(beside, next_along_y(across))

    halves.wait_recv()
    rest = [4, 1, 5, 2, 6, 3, 7]
    for near, far in zip(rest, reversed(rest), strict=True):
        chunk = jnp.where(z < 10, near, far)
        i = chunk - FIRST
        k = jnp.where(chunk < 4, chunk * NYC + 2, (chunk - 4) * NYC) + core
        send1[i] = (send0[core, chunk].astype(f32) + recv0[i].astype(f32)).astype(bf16)
        pl.when(place != k)(to_sum(send1.at[i], k).start)

    pl.semaphore_wait(beside, 3)
    signal(beyond, in_tm(across))
    pl.semaphore_wait(beyond, 1)
    gather = [
        pltpu.make_async_remote_copy(
            xall.at[tm], xall.at[tm], x_send.at[d], x_recv.at[d], in_tm(lax.rem(tm + d, SEG)), MESH
        )
        for d in range(1, SEG)
    ]
    for copy in gather:
        copy.start()

    def announce(semaphore):
        for d in range(1, SEG):
            signal(semaphore, in_tm(lax.rem(tm + d, SEG)))

    @pl.when(sums & (tm == owner))
    def _():
        announce(ready)
        pl.semaphore_wait(column, SIDE - SEG)
        announce(complete)

    @pl.when(sums)
    def _():

        @pl.when(jnp.logical_not(both))
        def _():
            others = recv1.at[pl.ds(0, SIDE - 1)]
            pltpu.make_async_copy(others, others, s1_recv).wait()
            total = send1[jnp.where(side == 1, z, z + 4) - FIRST].astype(f32)
            for i in range(2, PLACES, 2):
                total = total + recv1[i].astype(f32)
            mine[...] = total.astype(bf16)

        @pl.when(both)
        def _():
            others = recv1.at[pl.ds(0, PLACES - 1)]
            pltpu.make_async_copy(others, others, s1_recv).wait()
            total = send0[core, z].astype(f32)
            for i in range(1, PLACES):
                total = total + recv1[i].astype(f32)
            mine[...] = total.astype(bf16)

        pl.when(tm != owner)(lambda: pl.semaphore_wait(ready, 1))

        def spread(p):
            return pltpu.make_async_remote_copy(
                mine, parts.at[core, tm], s2_send, s2_recv.at[tm], {"tm": owner, "array": p}, MESH
            )

        for z_to in ORDER:
            if z_to == ORDER[2]:
                pl.when(tm != owner)(lambda: pl.semaphore_wait(complete, 1))
            for side_to in range(2):
                p = z_to * NYC + 2 * side_to
                if p < SUMS:
                    for q in (p + 1, p):
                        pl.when(jnp.logical_not((tm == owner) & (place == q)))(spread(q).start)
                else:
                    spread(p + core).start()
        pl.when(tm == owner)(lambda: pltpu.make_async_copy(mine, parts.at[core, tm], s2_recv.at[tm]).start())

    step = iota((SAMPLES, CH), 0)
    for copy in gather:
        copy.wait_recv()
    for g in range(SEG):
        x = xall[g].astype(f32).T
        later = jnp.where(step == SAMPLES - 1, 0.0, pltpu.roll(x, SAMPLES - 1, 0))
        earlier = jnp.where(step == 0, 0.0, pltpu.roll(x, 1, 0))
        rhs_up[g, :, :CH] = x.astype(bf16)
        rhs_up[g, :, CH:] = later.astype(bf16)
        rhs_down[g, :, :CH] = x.astype(bf16)
        rhs_down[g, :, CH:] = earlier.astype(bf16)

    swap = pltpu.make_async_remote_copy(
        parts.at[core], parts.at[core], s3_send, s3_recv, {"tm": tm, "array": other}, MESH
    )

    @pl.when(jnp.logical_not(sums))
    def _():
        for g in range(SEG):
            pltpu.make_async_copy(mine, mine, s2_recv.at[g]).wait()
        swap.start()
        swap.wait_recv()

    lane = iota((ROWS, 128), 1)
    none = jnp.zeros((ROWS, 128), bf16)

    def later(low, high):
        rows = []
        for i in range(UP):
            q = 2 * i
            lo, hi = (pltpu.roll(low, q, 1), pltpu.roll(high, q, 1)) if q else (low, high)
            rows.append(jnp.concatenate([jnp.where(lane < q, none, lo), jnp.where(lane < q, lo, hi)], 1))
        return jnp.concatenate(rows, 0)

    def earlier(low, high):
        rows = []
        for i in range(DOWN):
            q = 128 - (2 * i + 1)
            lo, hi = pltpu.roll(low, q, 1), pltpu.roll(high, q, 1)
            rows.append(jnp.concatenate([jnp.where(lane < q, lo, hi), jnp.where(lane < q, hi, none)], 1))
        return jnp.concatenate(rows, 0)

    order = [lax.rem(g, SEG) for g in (tm, right, left, across, tm + 4, across + 2, across + 6, across + 4)]
    pair = send1.at[pl.ds(0, 2)]
    rising = jnp.zeros((ROWS * UP, 2 * CH), f32)
    falling = jnp.zeros((ROWS * DOWN, 2 * CH), f32)
    for group in (order[: SEG // 2], order[SEG // 2 :]):

        @pl.when(sums)
        def _():
            for g in group:
                pltpu.make_async_copy(pair, pair, s2_recv.at[g]).wait()

        halves_of = []
        for g in group:
            one = parts[0, g].astype(f32)
            two = parts[1, g].astype(f32)
            low = jnp.concatenate([one[:8], two[:8]], 0).astype(bf16)
            high = jnp.concatenate([one[8:], two[8:]], 0).astype(bf16)
            halves_of.append((low, high))
        for g, lh in zip(group, halves_of, strict=True):
            rising = rising + jnp.dot(later(*lh), rhs_up[g], preferred_element_type=f32)
        if group[-1] is order[-1]:
            for i in range(UP):
                block = (rising[ROWS * i : ROWS * (i + 1)] * SCALE).astype(bf16)
                lag = MAXLAG + 2 * i
                out_ref[lag] = block[:, :CH]
                if lag + 1 < LAGS:
                    out_ref[lag + 1] = block[:, CH:]
        for g, lh in zip(group, halves_of, strict=True):
            falling = falling + jnp.dot(earlier(*lh), rhs_down[g], preferred_element_type=f32)

    for i in range(DOWN):
        block = (falling[ROWS * i : ROWS * (i + 1)] * SCALE).astype(bf16)
        lag = MAXLAG - 1 - 2 * i
        out_ref[lag] = block[:, :CH]
        out_ref[lag - 1] = block[:, CH:]

    for copy in gather + [halves]:
        copy.wait_send()

    pl.when(jnp.logical_not(sums))(swap.wait_send)

    @pl.when(jnp.logical_not(sums))
    def _():
        sent = recv1.at[pl.ds(0, SEG + FIRST)]
        pltpu.make_async_copy(sent, sent, s1_send).wait()

    @pl.when(sums)
    def _():
        sent = recv1.at[pl.ds(0, SEG + FIRST - 1)]
        pltpu.make_async_copy(sent, sent, s1_send).wait()
        users = recv1.at[pl.ds(0, USERS)]
        others = recv1.at[pl.ds(0, USERS - 1)]
        pl.when(tm != owner)(lambda: pltpu.make_async_copy(users, users, s2_send).wait())
        pl.when(tm == owner)(lambda: pltpu.make_async_copy(others, others, s2_send).wait())


def body(raw_strain, fir_taps, source_ids):
    hbm = pl.BlockSpec(memory_space=pltpu.HBM)
    dma = pltpu.SemaphoreType.DMA
    signals = pltpu.SemaphoreType.REGULAR
    out = pl.pallas_call(
        kernel,
        out_shape=pltpu.VMEM((LAGS, ROWS, CH), bf16),
        in_specs=[hbm, hbm, hbm],
        out_specs=pl.BlockSpec(memory_space=pltpu.VMEM),
        scratch_shapes=[
            pltpu.VMEM((1, CH, RAW), bf16),
            pltpu.SMEM((NTAP,), f32),
            pltpu.VMEM((4, 32), jnp.int32),
            pltpu.VMEM((SEG, CH, SAMPLES), bf16),
            pltpu.VMEM((2, SEG, 16, 128), bf16),
            pltpu.VMEM((SEG - FIRST, 16, 128), bf16),
            pltpu.VMEM((SEG - FIRST, 16, 128), bf16),
            pltpu.VMEM((PLACES, 16, 128), bf16),
            pltpu.VMEM((16, 128), bf16),
            pltpu.VMEM((2, SEG, 16, 128), bf16),
            pltpu.VMEM((SEG, SAMPLES, 2 * CH), bf16),
            pltpu.VMEM((SEG, SAMPLES, 2 * CH), bf16),
            dma((3,)),
            dma((SEG,)), dma((SEG,)),
            dma, dma,
            dma, dma,
            dma, dma((SEG,)),
            dma, dma,
            signals, signals, signals, signals, signals,
        ],
        compiler_params=pltpu.CompilerParams(
            collective_id=0, has_side_effects=True, vmem_limit_bytes=56 * 1024 * 1024
        ),
    )(raw_strain, fir_taps, source_ids)
    return out.transpose(1, 0, 2)


def solution(mesh):
    return jax.shard_map(
        body,
        mesh=mesh,
        in_specs=(P("tm", "array", None), P(), P()),
        out_specs=P("tm", None, "array"),
        check_vma=False,
    )
```

```python
import functools
import math

import jax
import jax.numpy as jnp
from jax import lax
from jax.experimental import pallas as pl
from jax.experimental.pallas import tpu as pltpu
from jax.sharding import PartitionSpec as P

MESH = pl.DeviceIdType.MESH
SOURCES = 128
MAXLAG = 50
WINDOW = 64
DECIM = 4
NTAP = 8
SAMPLES = 256
LAGS = 101
RAW = 1024
SEG = 8
ROWS = 16
CH = 128
NZ = 16
NYC = 4
PLACES = NZ * NYC
FIRST = 1
SUMS = 16
SIDE = PLACES // 2
ORDER = (0, 1, 4, 5, 2, 6, 9, 10, 3, 7, 8, 11, 12, 13, 14, 15)
USERS = SUMS + (PLACES - SUMS) // 2
UP = 26
DOWN = 25
EPSILON = 1e-05
SCALE = 1.0 / (math.sqrt(SAMPLES) * math.sqrt(SEG))

f32 = jnp.float32
bf16 = jnp.bfloat16
TN = (((0,), (0,)), ((), ()))


def iota(shape, dim):
    return lax.broadcasted_iota(jnp.int32, shape, dim)


def terms(value, count):
    parts = []
    for _ in range(count):
        part = value.astype(bf16)
        parts.append(part)
        value = value - part.astype(f32)
    return parts


def tap_bands(taps_ref):
    k = DECIM * iota((128, 128), 1) - iota((128, 128), 0)
    band = jnp.zeros((128, 128), f32)
    for tap in range(NTAP):
        band = jnp.where(k == tap, taps_ref[tap], band)
    band = jnp.concatenate([band, jnp.zeros((128, 128), f32)], 1)
    lane = iota((128, SAMPLES), 1)
    bands = []
    for tile in range(RAW // 128):
        placed = pltpu.roll(band, 32 * tile, 1) if tile else band
        if tile == RAW // 128 - 1:
            placed = jnp.where(lane < 2, 0.0, placed)
        bands.append(terms(placed, 3))
    return bands


def decimate(raw, bands):
    filtered = jnp.zeros((CH, SAMPLES), f32)
    for term in range(3):
        matrix = jnp.concatenate([band[term] for band in bands], 0)
        filtered = filtered + jnp.dot(raw, matrix, preferred_element_type=f32)
    return filtered


def window_matrix():
    gap = iota((SAMPLES, SAMPLES), 0) - iota((SAMPLES, SAMPLES), 1)
    return jnp.where((gap >= -(WINDOW // 2)) & (gap < WINDOW // 2), 1.0, 0.0).astype(bf16)


def normalize(filtered, window):
    total = jnp.zeros((CH, SAMPLES), f32)
    for part in terms(jnp.abs(filtered), 2):
        total = total + jnp.dot(part, window, preferred_element_type=f32)
    return filtered / (total * (1.0 / WINDOW) + EPSILON)


def kernel(
    raw_hbm, taps_hbm, ids_hbm, out_ref,
    raw, taps, ids_ref, xall, send0, recv0, send1, recv1, mine, parts, rhs_up, rhs_down,
    in_sem, x_send, x_recv, s0_send, s0_recv, s1_send, s1_recv, s2_send, s2_recv, s3_send, s3_recv, column, beside, beyond, ready, complete,
):
    inputs = [
        pltpu.make_async_copy(src, dst, in_sem.at[i])
        for i, (src, dst) in enumerate(((raw_hbm, raw), (taps_hbm, taps), (ids_hbm, ids_ref)))
    ]
    for copy in inputs:
        copy.start()

    tm = lax.axis_index("tm")
    place = lax.axis_index("array")
    z = lax.div(place, NYC)
    core = lax.rem(place, 2)
    side = lax.rem(lax.div(place, 2), 2)
    other = place + 1 - 2 * core
    sums = place < SUMS
    owner = 2 * z + 1 - side
    both = sums & (side == 1) & (z < FIRST)

    right, left = lax.rem(tm + 2, SEG), lax.rem(tm + 6, SEG)
    across = tm + 1 - 2 * lax.rem(tm, 2)

    beyond_side = place + 2 - 4 * side

    def in_tm(t):
        return {"tm": t, "array": place}

    def next_along_y(t):
        return {"tm": t, "array": beyond_side}

    def signal(semaphore, device):
        pl.semaphore_signal(semaphore, inc=1, device_id=device, device_id_type=MESH)

    barrier = pltpu.get_barrier_semaphore()
    for t in (left, right):
        signal(barrier, in_tm(t))
    for t in (tm, across):
        signal(barrier, next_along_y(t))
    pl.when(jnp.logical_not(sums))(lambda: signal(barrier, {"tm": tm, "array": other}))

    @pl.when(sums)
    def _():
        def greet(d, carry):
            signal(barrier, {"tm": tm, "array": lax.rem(place + 2 * d, PLACES)})
            return carry

        def greet_other(d, carry):
            signal(barrier, {"tm": tm, "array": lax.rem(other + 2 * d, PLACES)})
            return carry

        @pl.when(jnp.logical_not(both))
        def _():
            for k in range(0, SUMS, 2):
                signal(barrier, {"tm": tm, "array": k + 1 - core})

        @pl.when(both)
        def _():
            lax.fori_loop(0, SIDE, greet_other, 0)

        lax.fori_loop(1, SIDE, greet, 0)

    inputs[1].wait()
    bands = tap_bands(taps)

    window = window_matrix()

    inputs[2].wait()
    ids = jnp.concatenate([ids_ref[r : r + 1, :] for r in range(4)], 1)
    chosen = (iota((CH, SOURCES), 0) == ids - place * CH).astype(f32).astype(bf16)

    inputs[0].wait()
    filtered = decimate(raw[0], bands)

    pl.semaphore_wait(barrier, jnp.where(sums, SUMS - 1, SEG + FIRST + 1) + 4)

    mine_at = lax.div(tm, 2) * NYC + 2 * (1 - lax.rem(tm, 2)) + core
    pl.when(jnp.logical_not(sums))(lambda: signal(column, {"tm": tm, "array": mine_at}))

    xall[tm] = normalize(filtered, window).astype(bf16)

    picked = lax.dot_general(chosen, xall[tm], TN, preferred_element_type=f32)
    for t in range(SEG):
        for h in range(2):
            part = picked[ROWS * t + 8 * h : ROWS * t + 8 * h + 8]
            send0[h, t // 2 + 4 * (t % 2)] = jnp.concatenate([part[:, :128], part[:, 128:]], 0).astype(bf16)

    halves = pltpu.make_async_remote_copy(
        send0.at[1 - core, pl.ds(FIRST, SEG - FIRST)], recv0, s0_send, s0_recv, {"tm": tm, "array": other}, MESH
    )

    def to_sum(chunk, k):
        slot = lax.rem(place - k + PLACES, PLACES)
        return pltpu.make_async_remote_copy(
            chunk, recv1.at[slot], s1_send, s1_recv, {"tm": tm, "array": k}, MESH
        )

    for plane in range(FIRST):
        k = plane * NYC + 2 + core
        pl.when(place != k)(to_sum(send0.at[core, plane], k).start)
        to_sum(send0.at[1 - core, plane], plane * NYC + 3 - core).start()

    halves.start()

    signal(beside, in_tm(left))
    signal(beside, next_along_y(tm))
    signal(beside, next_along_y(across))

    halves.wait_recv()
    rest = [4, 1, 5, 2, 6, 3, 7]
    for near, far in zip(rest, reversed(rest), strict=True):
        chunk = jnp.where(z < 10, near, far)
        i = chunk - FIRST
        k = jnp.where(chunk < 4, chunk * NYC + 2, (chunk - 4) * NYC) + core
        send1[i] = (send0[core, chunk].astype(f32) + recv0[i].astype(f32)).astype(bf16)
        pl.when(place != k)(to_sum(send1.at[i], k).start)

    pl.semaphore_wait(beside, 3)
    signal(beyond, in_tm(across))
    pl.semaphore_wait(beyond, 1)
    gather = [
        pltpu.make_async_remote_copy(
            xall.at[tm], xall.at[tm], x_send.at[d], x_recv.at[d], in_tm(lax.rem(tm + d, SEG)), MESH
        )
        for d in range(1, SEG)
    ]
    for copy in gather:
        copy.start()

    def announce(semaphore):
        for d in range(1, SEG):
            signal(semaphore, in_tm(lax.rem(tm + d, SEG)))

    @pl.when(sums & (tm == owner))
    def _():
        announce(ready)
        pl.semaphore_wait(column, SIDE - SEG)
        announce(complete)

    @pl.when(sums)
    def _():

        @pl.when(jnp.logical_not(both))
        def _():
            others = recv1.at[pl.ds(0, SIDE - 1)]
            pltpu.make_async_copy(others, others, s1_recv).wait()
            total = send1[jnp.where(side == 1, z, z + 4) - FIRST].astype(f32)
            for i in range(2, PLACES, 2):
                total = total + recv1[i].astype(f32)
            mine[...] = total.astype(bf16)

        @pl.when(both)
        def _():
            others = recv1.at[pl.ds(0, PLACES - 1)]
            pltpu.make_async_copy(others, others, s1_recv).wait()
            total = send0[core, z].astype(f32)
            for i in range(1, PLACES):
                total = total + recv1[i].astype(f32)
            mine[...] = total.astype(bf16)

        pl.when(tm != owner)(lambda: pl.semaphore_wait(ready, 1))

        def spread(p):
            return pltpu.make_async_remote_copy(
                mine, parts.at[core, tm], s2_send, s2_recv.at[tm], {"tm": owner, "array": p}, MESH
            )

        for z_to in ORDER:
            if z_to == ORDER[2]:
                pl.when(tm != owner)(lambda: pl.semaphore_wait(complete, 1))
            for side_to in range(2):
                p = z_to * NYC + 2 * side_to
                if p < SUMS:
                    for q in (p + 1, p):
                        pl.when(jnp.logical_not((tm == owner) & (place == q)))(spread(q).start)
                else:
                    spread(p + core).start()
        pl.when(tm == owner)(lambda: pltpu.make_async_copy(mine, parts.at[core, tm], s2_recv.at[tm]).start())

    step = iota((SAMPLES, CH), 0)
    for copy in gather:
        copy.wait_recv()
    for g in range(SEG):
        x = xall[g].astype(f32).T
        later = jnp.where(step == SAMPLES - 1, 0.0, pltpu.roll(x, SAMPLES - 1, 0))
        earlier = jnp.where(step == 0, 0.0, pltpu.roll(x, 1, 0))
        rhs_up[g, :, :CH] = x.astype(bf16)
        rhs_up[g, :, CH:] = later.astype(bf16)
        rhs_down[g, :, :CH] = x.astype(bf16)
        rhs_down[g, :, CH:] = earlier.astype(bf16)

    swap = pltpu.make_async_remote_copy(
        parts.at[core], parts.at[core], s3_send, s3_recv, {"tm": tm, "array": other}, MESH
    )

    @pl.when(jnp.logical_not(sums))
    def _():
        for g in range(SEG):
            pltpu.make_async_copy(mine, mine, s2_recv.at[g]).wait()
        swap.start()
        swap.wait_recv()

    lane = iota((ROWS, 128), 1)
    none = jnp.zeros((ROWS, 128), bf16)

    def later(low, high):
        rows = []
        for i in range(UP):
            q = 2 * i
            lo, hi = (pltpu.roll(low, q, 1), pltpu.roll(high, q, 1)) if q else (low, high)
            rows.append(jnp.concatenate([jnp.where(lane < q, none, lo), jnp.where(lane < q, lo, hi)], 1))
        return jnp.concatenate(rows, 0)

    def earlier(low, high):
        rows = []
        for i in range(DOWN):
            q = 128 - (2 * i + 1)
            lo, hi = pltpu.roll(low, q, 1), pltpu.roll(high, q, 1)
            rows.append(jnp.concatenate([jnp.where(lane < q, lo, hi), jnp.where(lane < q, hi, none)], 1))
        return jnp.concatenate(rows, 0)

    order = [lax.rem(g, SEG) for g in (tm, right, left, across, tm + 4, across + 2, across + 6, across + 4)]
    pair = send1.at[pl.ds(0, 2)]
    rising = jnp.zeros((ROWS * UP, 2 * CH), f32)
    falling = jnp.zeros((ROWS * DOWN, 2 * CH), f32)
    for group in (order[: SEG // 2], order[SEG // 2 :]):

        @pl.when(sums)
        def _():
            for g in group:
                pltpu.make_async_copy(pair, pair, s2_recv.at[g]).wait()

        halves_of = []
        for g in group:
            one = parts[0, g].astype(f32)
            two = parts[1, g].astype(f32)
            low = jnp.concatenate([one[:8], two[:8]], 0).astype(bf16)
            high = jnp.concatenate([one[8:], two[8:]], 0).astype(bf16)
            halves_of.append((low, high))
        for g, lh in zip(group, halves_of, strict=True):
            rising = rising + jnp.dot(later(*lh), rhs_up[g], preferred_element_type=f32)
        if group[-1] is order[-1]:
            for i in range(UP):
                block = (rising[ROWS * i : ROWS * (i + 1)] * SCALE).astype(bf16)
                lag = MAXLAG + 2 * i
                out_ref[lag] = block[:, :CH]
                if lag + 1 < LAGS:
                    out_ref[lag + 1] = block[:, CH:]
        for g, lh in zip(group, halves_of, strict=True):
            falling = falling + jnp.dot(earlier(*lh), rhs_down[g], preferred_element_type=f32)

    for i in range(DOWN):
        block = (falling[ROWS * i : ROWS * (i + 1)] * SCALE).astype(bf16)
        lag = MAXLAG - 1 - 2 * i
        out_ref[lag] = block[:, :CH]
        out_ref[lag - 1] = block[:, CH:]

    for copy in gather + [halves]:
        copy.wait_send()

    pl.when(jnp.logical_not(sums))(swap.wait_send)

    @pl.when(jnp.logical_not(sums))
    def _():
        sent = recv1.at[pl.ds(0, SEG + FIRST)]
        pltpu.make_async_copy(sent, sent, s1_send).wait()

    @pl.when(sums)
    def _():
        sent = recv1.at[pl.ds(0, SEG + FIRST - 1)]
        pltpu.make_async_copy(sent, sent, s1_send).wait()
        users = recv1.at[pl.ds(0, USERS)]
        others = recv1.at[pl.ds(0, USERS - 1)]
        pl.when(tm != owner)(lambda: pltpu.make_async_copy(users, users, s2_send).wait())
        pl.when(tm == owner)(lambda: pltpu.make_async_copy(others, others, s2_send).wait())


def body(raw_strain, fir_taps, source_ids):
    hbm = pl.BlockSpec(memory_space=pltpu.HBM)
    dma = pltpu.SemaphoreType.DMA
    signals = pltpu.SemaphoreType.REGULAR
    out = pl.pallas_call(
        kernel,
        out_shape=pltpu.VMEM((LAGS, ROWS, CH), bf16),
        in_specs=[hbm, hbm, hbm],
        out_specs=pl.BlockSpec(memory_space=pltpu.VMEM),
        scratch_shapes=[
            pltpu.VMEM((1, CH, RAW), bf16),
            pltpu.SMEM((NTAP,), f32),
            pltpu.VMEM((4, 32), jnp.int32),
            pltpu.VMEM((SEG, CH, SAMPLES), bf16),
            pltpu.VMEM((2, SEG, 16, 128), bf16),
            pltpu.VMEM((SEG - FIRST, 16, 128), bf16),
            pltpu.VMEM((SEG - FIRST, 16, 128), bf16),
            pltpu.VMEM((PLACES, 16, 128), bf16),
            pltpu.VMEM((16, 128), bf16),
            pltpu.VMEM((2, SEG, 16, 128), bf16),
            pltpu.VMEM((SEG, SAMPLES, 2 * CH), bf16),
            pltpu.VMEM((SEG, SAMPLES, 2 * CH), bf16),
            dma((3,)),
            dma((SEG,)), dma((SEG,)),
            dma, dma,
            dma, dma,
            dma, dma((SEG,)),
            dma, dma,
            signals, signals, signals, signals, signals,
        ],
        compiler_params=pltpu.CompilerParams(
            collective_id=0, has_side_effects=True, vmem_limit_bytes=56 * 1024 * 1024
        ),
    )(raw_strain, fir_taps, source_ids)
    return out.transpose(1, 0, 2)


def solution(mesh):
    return jax.shard_map(
        body,
        mesh=mesh,
        in_specs=(P("tm", "array", None), P(), P()),
        out_specs=P("tm", None, "array"),
        check_vma=False,
    )
```

```python
import functools
import math

import jax
import jax.numpy as jnp
from jax import lax
from jax.experimental import pallas as pl
from jax.experimental.pallas import tpu as pltpu
from jax.sharding import PartitionSpec as P

MESH = pl.DeviceIdType.MESH
SOURCES = 128
MAXLAG = 50
WINDOW = 64
DECIM = 4
NTAP = 8
SAMPLES = 256
LAGS = 101
RAW = 1024
SEG = 8
ROWS = 16
CH = 128
NZ = 16
NYC = 4
PLACES = NZ * NYC
FIRST = 1
SUMS = 16
SIDE = PLACES // 2
ORDER = (0, 1, 4, 5, 2, 6, 9, 10, 3, 7, 8, 11, 12, 13, 14, 15)
USERS = SUMS + (PLACES - SUMS) // 2
UP = 26
DOWN = 25
EPSILON = 1e-05
SCALE = 1.0 / (math.sqrt(SAMPLES) * math.sqrt(SEG))

f32 = jnp.float32
bf16 = jnp.bfloat16
TN = (((0,), (0,)), ((), ()))


def iota(shape, dim):
    return lax.broadcasted_iota(jnp.int32, shape, dim)


def terms(value, count):
    parts = []
    for _ in range(count):
        part = value.astype(bf16)
        parts.append(part)
        value = value - part.astype(f32)
    return parts


def tap_bands(taps_ref):
    k = DECIM * iota((128, 128), 1) - iota((128, 128), 0)
    band = jnp.zeros((128, 128), f32)
    for tap in range(NTAP):
        band = jnp.where(k == tap, taps_ref[tap], band)
    band = jnp.concatenate([band, jnp.zeros((128, 128), f32)], 1)
    lane = iota((128, SAMPLES), 1)
    bands = []
    for tile in range(RAW // 128):
        placed = pltpu.roll(band, 32 * tile, 1) if tile else band
        if tile == RAW // 128 - 1:
            placed = jnp.where(lane < 2, 0.0, placed)
        bands.append(terms(placed, 3))
    return bands


def decimate(raw, bands):
    filtered = jnp.zeros((CH, SAMPLES), f32)
    for term in range(3):
        matrix = jnp.concatenate([band[term] for band in bands], 0)
        filtered = filtered + jnp.dot(raw, matrix, preferred_element_type=f32)
    return filtered


def window_matrix():
    gap = iota((SAMPLES, SAMPLES), 0) - iota((SAMPLES, SAMPLES), 1)
    return jnp.where((gap >= -(WINDOW // 2)) & (gap < WINDOW // 2), 1.0, 0.0).astype(bf16)


def normalize(filtered, window):
    total = jnp.zeros((CH, SAMPLES), f32)
    for part in terms(jnp.abs(filtered), 2):
        total = total + jnp.dot(part, window, preferred_element_type=f32)
    return filtered / (total * (1.0 / WINDOW) + EPSILON)


def kernel(
    raw_hbm, taps_hbm, ids_hbm, out_ref,
    raw, taps, ids_ref, xall, send0, recv0, send1, recv1, mine, parts, rhs_up, rhs_down,
    in_sem, x_send, x_recv, s0_send, s0_recv, s1_send, s1_recv, s2_send, s2_recv, s3_send, s3_recv, column, beside, beyond, ready, complete,
):
    inputs = [
        pltpu.make_async_copy(src, dst, in_sem.at[i])
        for i, (src, dst) in enumerate(((raw_hbm, raw), (taps_hbm, taps), (ids_hbm, ids_ref)))
    ]
    for copy in inputs:
        copy.start()

    tm = lax.axis_index("tm")
    place = lax.axis_index("array")
    z = lax.div(place, NYC)
    core = lax.rem(place, 2)
    side = lax.rem(lax.div(place, 2), 2)
    other = place + 1 - 2 * core
    sums = place < SUMS
    owner = 2 * z + 1 - side
    both = sums & (side == 1) & (z < FIRST)

    right, left = lax.rem(tm + 2, SEG), lax.rem(tm + 6, SEG)
    across = tm + 1 - 2 * lax.rem(tm, 2)

    beyond_side = place + 2 - 4 * side

    def in_tm(t):
        return {"tm": t, "array": place}

    def next_along_y(t):
        return {"tm": t, "array": beyond_side}

    def signal(semaphore, device):
        pl.semaphore_signal(semaphore, inc=1, device_id=device, device_id_type=MESH)

    barrier = pltpu.get_barrier_semaphore()
    for t in (left, right):
        signal(barrier, in_tm(t))
    for t in (tm, across):
        signal(barrier, next_along_y(t))
    pl.when(jnp.logical_not(sums))(lambda: signal(barrier, {"tm": tm, "array": other}))

    @pl.when(sums)
    def _():
        def greet(d, carry):
            signal(barrier, {"tm": tm, "array": lax.rem(place + 2 * d, PLACES)})
            return carry

        def greet_other(d, carry):
            signal(barrier, {"tm": tm, "array": lax.rem(other + 2 * d, PLACES)})
            return carry

        @pl.when(jnp.logical_not(both))
        def _():
            for k in range(0, SUMS, 2):
                signal(barrier, {"tm": tm, "array": k + 1 - core})

        @pl.when(both)
        def _():
            lax.fori_loop(0, SIDE, greet_other, 0)

        lax.fori_loop(1, SIDE, greet, 0)

    inputs[1].wait()
    bands = tap_bands(taps)

    window = window_matrix()

    inputs[2].wait()
    ids = jnp.concatenate([ids_ref[r : r + 1, :] for r in range(4)], 1)
    chosen = (iota((CH, SOURCES), 0) == ids - place * CH).astype(f32).astype(bf16)

    inputs[0].wait()
    filtered = decimate(raw[0], bands)

    pl.semaphore_wait(barrier, jnp.where(sums, SUMS - 1, SEG + FIRST + 1) + 4)

    mine_at = lax.div(tm, 2) * NYC + 2 * (1 - lax.rem(tm, 2)) + core
    pl.when(jnp.logical_not(sums))(lambda: signal(column, {"tm": tm, "array": mine_at}))

    xall[tm] = normalize(filtered, window).astype(bf16)

    picked = lax.dot_general(chosen, xall[tm], TN, preferred_element_type=f32)
    for t in range(SEG):
        for h in range(2):
            part = picked[ROWS * t + 8 * h : ROWS * t + 8 * h + 8]
            send0[h, t // 2 + 4 * (t % 2)] = jnp.concatenate([part[:, :128], part[:, 128:]], 0).astype(bf16)

    halves = pltpu.make_async_remote_copy(
        send0.at[1 - core, pl.ds(FIRST, SEG - FIRST)], recv0, s0_send, s0_recv, {"tm": tm, "array": other}, MESH
    )
    halves.start()

    def to_sum(chunk, k):
        slot = lax.rem(place - k + PLACES, PLACES)
        return pltpu.make_async_remote_copy(
            chunk, recv1.at[slot], s1_send, s1_recv, {"tm": tm, "array": k}, MESH
        )

    for plane in range(FIRST):
        k = plane * NYC + 2 + core
        pl.when(place != k)(to_sum(send0.at[core, plane], k).start)
        to_sum(send0.at[1 - core, plane], plane * NYC + 3 - core).start()

    signal(beside, in_tm(left))
    signal(beside, next_along_y(tm))
    signal(beside, next_along_y(across))

    halves.wait_recv()
    rest = [4, 1, 5, 2, 6, 3, 7]
    for near, far in zip(rest, reversed(rest), strict=True):
        chunk = jnp.where(z < 10, near, far)
        i = chunk - FIRST
        k = jnp.where(chunk < 4, chunk * NYC + 2, (chunk - 4) * NYC) + core
        send1[i] = (send0[core, chunk].astype(f32) + recv0[i].astype(f32)).astype(bf16)
        pl.when(place != k)(to_sum(send1.at[i], k).start)

    pl.semaphore_wait(beside, 3)
    signal(beyond, in_tm(across))
    pl.semaphore_wait(beyond, 1)
    gather = [
        pltpu.make_async_remote_copy(
            xall.at[tm], xall.at[tm], x_send.at[d], x_recv.at[d], in_tm(lax.rem(tm + d, SEG)), MESH
        )
        for d in range(1, SEG)
    ]
    for copy in gather:
        copy.start()

    def announce(semaphore):
        for d in range(1, SEG):
            signal(semaphore, in_tm(lax.rem(tm + d, SEG)))

    @pl.when(sums & (tm == owner))
    def _():
        announce(ready)
        pl.semaphore_wait(column, SIDE - SEG)
        announce(complete)

    @pl.when(sums)
    def _():

        @pl.when(jnp.logical_not(both))
        def _():
            others = recv1.at[pl.ds(0, SIDE - 1)]
            pltpu.make_async_copy(others, others, s1_recv).wait()
            total = send1[jnp.where(side == 1, z, z + 4) - FIRST].astype(f32)
            for i in range(2, PLACES, 2):
                total = total + recv1[i].astype(f32)
            mine[...] = total.astype(bf16)

        @pl.when(both)
        def _():
            others = recv1.at[pl.ds(0, PLACES - 1)]
            pltpu.make_async_copy(others, others, s1_recv).wait()
            total = send0[core, z].astype(f32)
            for i in range(1, PLACES):
                total = total + recv1[i].astype(f32)
            mine[...] = total.astype(bf16)

        pl.when(tm != owner)(lambda: pl.semaphore_wait(ready, 1))

        def spread(p):
            return pltpu.make_async_remote_copy(
                mine, parts.at[core, tm], s2_send, s2_recv.at[tm], {"tm": owner, "array": p}, MESH
            )

        for z_to in ORDER:
            if z_to == ORDER[2]:
                pl.when(tm != owner)(lambda: pl.semaphore_wait(complete, 1))
            for side_to in range(2):
                p = z_to * NYC + 2 * side_to
                if p < SUMS:
                    for q in (p + 1, p):
                        pl.when(jnp.logical_not((tm == owner) & (place == q)))(spread(q).start)
                else:
                    spread(p + core).start()
        pl.when(tm == owner)(lambda: pltpu.make_async_copy(mine, parts.at[core, tm], s2_recv.at[tm]).start())

    step = iota((SAMPLES, CH), 0)
    for copy in gather:
        copy.wait_recv()
    for g in range(SEG):
        x = xall[g].astype(f32).T
        later = jnp.where(step == SAMPLES - 1, 0.0, pltpu.roll(x, SAMPLES - 1, 0))
        earlier = jnp.where(step == 0, 0.0, pltpu.roll(x, 1, 0))
        rhs_up[g, :, :CH] = x.astype(bf16)
        rhs_up[g, :, CH:] = later.astype(bf16)
        rhs_down[g, :, :CH] = x.astype(bf16)
        rhs_down[g, :, CH:] = earlier.astype(bf16)

    swap = pltpu.make_async_remote_copy(
        parts.at[core], parts.at[core], s3_send, s3_recv, {"tm": tm, "array": other}, MESH
    )

    @pl.when(jnp.logical_not(sums))
    def _():
        for g in range(SEG):
            pltpu.make_async_copy(mine, mine, s2_recv.at[g]).wait()
        swap.start()
        swap.wait_recv()

    lane = iota((ROWS, 128), 1)
    none = jnp.zeros((ROWS, 128), bf16)

    def later(low, high):
        rows = []
        for i in range(UP):
            q = 2 * i
            lo, hi = (pltpu.roll(low, q, 1), pltpu.roll(high, q, 1)) if q else (low, high)
            rows.append(jnp.concatenate([jnp.where(lane < q, none, lo), jnp.where(lane < q, lo, hi)], 1))
        return jnp.concatenate(rows, 0)

    def earlier(low, high):
        rows = []
        for i in range(DOWN):
            q = 128 - (2 * i + 1)
            lo, hi = pltpu.roll(low, q, 1), pltpu.roll(high, q, 1)
            rows.append(jnp.concatenate([jnp.where(lane < q, lo, hi), jnp.where(lane < q, hi, none)], 1))
        return jnp.concatenate(rows, 0)

    order = [lax.rem(g, SEG) for g in (tm, right, left, across, tm + 4, across + 2, across + 6, across + 4)]
    pair = send1.at[pl.ds(0, 2)]
    rising = jnp.zeros((ROWS * UP, 2 * CH), f32)
    falling = jnp.zeros((ROWS * DOWN, 2 * CH), f32)
    for group in (order[:5], order[5:]):

        @pl.when(sums)
        def _():
            for g in group:
                pltpu.make_async_copy(pair, pair, s2_recv.at[g]).wait()

        halves_of = []
        for g in group:
            one = parts[0, g].astype(f32)
            two = parts[1, g].astype(f32)
            low = jnp.concatenate([one[:8], two[:8]], 0).astype(bf16)
            high = jnp.concatenate([one[8:], two[8:]], 0).astype(bf16)
            halves_of.append((low, high))
        for g, lh in zip(group, halves_of, strict=True):
            rising = rising + jnp.dot(later(*lh), rhs_up[g], preferred_element_type=f32)
        if group[-1] is order[-1]:
            for i in range(UP):
                block = (rising[ROWS * i : ROWS * (i + 1)] * SCALE).astype(bf16)
                lag = MAXLAG + 2 * i
                out_ref[lag] = block[:, :CH]
                if lag + 1 < LAGS:
                    out_ref[lag + 1] = block[:, CH:]
        for g, lh in zip(group, halves_of, strict=True):
            falling = falling + jnp.dot(earlier(*lh), rhs_down[g], preferred_element_type=f32)

    for i in range(DOWN):
        block = (falling[ROWS * i : ROWS * (i + 1)] * SCALE).astype(bf16)
        lag = MAXLAG - 1 - 2 * i
        out_ref[lag] = block[:, :CH]
        out_ref[lag - 1] = block[:, CH:]

    for copy in gather + [halves]:
        copy.wait_send()

    pl.when(jnp.logical_not(sums))(swap.wait_send)

    @pl.when(jnp.logical_not(sums))
    def _():
        sent = recv1.at[pl.ds(0, SEG + FIRST)]
        pltpu.make_async_copy(sent, sent, s1_send).wait()

    @pl.when(sums)
    def _():
        sent = recv1.at[pl.ds(0, SEG + FIRST - 1)]
        pltpu.make_async_copy(sent, sent, s1_send).wait()
        users = recv1.at[pl.ds(0, USERS)]
        others = recv1.at[pl.ds(0, USERS - 1)]
        pl.when(tm != owner)(lambda: pltpu.make_async_copy(users, users, s2_send).wait())
        pl.when(tm == owner)(lambda: pltpu.make_async_copy(others, others, s2_send).wait())


def body(raw_strain, fir_taps, source_ids):
    hbm = pl.BlockSpec(memory_space=pltpu.HBM)
    dma = pltpu.SemaphoreType.DMA
    signals = pltpu.SemaphoreType.REGULAR
    out = pl.pallas_call(
        kernel,
        out_shape=pltpu.VMEM((LAGS, ROWS, CH), bf16),
        in_specs=[hbm, hbm, hbm],
        out_specs=pl.BlockSpec(memory_space=pltpu.VMEM),
        scratch_shapes=[
            pltpu.VMEM((1, CH, RAW), bf16),
            pltpu.SMEM((NTAP,), f32),
            pltpu.VMEM((4, 32), jnp.int32),
            pltpu.VMEM((SEG, CH, SAMPLES), bf16),
            pltpu.VMEM((2, SEG, 16, 128), bf16),
            pltpu.VMEM((SEG - FIRST, 16, 128), bf16),
            pltpu.VMEM((SEG - FIRST, 16, 128), bf16),
            pltpu.VMEM((PLACES, 16, 128), bf16),
            pltpu.VMEM((16, 128), bf16),
            pltpu.VMEM((2, SEG, 16, 128), bf16),
            pltpu.VMEM((SEG, SAMPLES, 2 * CH), bf16),
            pltpu.VMEM((SEG, SAMPLES, 2 * CH), bf16),
            dma((3,)),
            dma((SEG,)), dma((SEG,)),
            dma, dma,
            dma, dma,
            dma, dma((SEG,)),
            dma, dma,
            signals, signals, signals, signals, signals,
        ],
        compiler_params=pltpu.CompilerParams(
            collective_id=0, has_side_effects=True, vmem_limit_bytes=56 * 1024 * 1024
        ),
    )(raw_strain, fir_taps, source_ids)
    return out.transpose(1, 0, 2)


def solution(mesh):
    return jax.shard_map(
        body,
        mesh=mesh,
        in_specs=(P("tm", "array", None), P(), P()),
        out_specs=P("tm", None, "array"),
        check_vma=False,
    )
```
